128 devices in a mesh: section: 2 (over y_hi), seq: 16 (over z, y_lo, core), mp: 4 (over x).
Axes of the slice: x: 4, y: 4 (y_hi: 2, y_lo: 2; y = y_hi * 2 + y_lo), z: 4, core: 2. Of those that a mesh axis runs over, the one named last changes fastest.
Arguments:
- patches: bfloat16 [16384, 1280], P('seq'), may hold values from -6 to 6
- norm_gain: bfloat16 [1280], replicated, may hold values from 0.099609375 to 1.8984375
- norm_shift: bfloat16 [1280], replicated, may hold values from -3 to 3
- merge_in_weight: bfloat16 [5120, 5120], P(None, ('section', 'mp')), may hold values from -0.078125 to 0.078125
- merge_in_bias: bfloat16 [5120], P(('section', 'mp')), may hold values from -3 to 3
- merge_out_weight: bfloat16 [5120, 8192], P(('section', 'mp'), 'seq'), may hold values from -0.078125 to 0.078125
- merge_out_bias: bfloat16 [8192], P('seq'), may hold values from -3 to 3
- text_embeds: bfloat16 [6144, 8192], P('seq', 'mp'), may hold values from -6 to 6
- rms_gain: bfloat16 [8192], replicated, may hold values from 0.099609375 to 1.8984375
- query_weight: bfloat16 [8192, 4096], P(None, ('section', 'mp')), may hold values from -0.0625 to 0.0625
- query_bias: bfloat16 [4096], P(('section', 'mp')), may hold values from -12 to 12
- key_weight: bfloat16 [8192, 512], P(None, 'mp'), may hold values from -0.0625 to 0.0625
- key_bias: bfloat16 [512], P('mp'), may hold values from -12 to 12
- value_weight: bfloat16 [8192, 512], P(None, 'mp'), may hold values from -0.0625 to 0.0625
- value_bias: bfloat16 [512], P('mp'), may hold values from -3 to 3
- patch_counts: int32 [16], replicated, may hold values from 256 to 1024, as said below
- image_offsets: int32 [16], replicated, may hold values from 0 to 6080, as said below
Outputs:
- sequence_embeds: bfloat16 [6144, 8192], P('seq', 'mp')
- context: bfloat16 [6144, 4096], P('seq', ('section', 'mp'))
The draws below stay inside these ranges and needn't reach their ends.
Inputs may be any that keep to these rules, and one draw needn't show every extreme that they name: `patch_counts`: multiples of 4; in every draw one image has exactly 1024 patches and another exactly a quarter of 1024. Image i's merged tokens occupy positions image_offsets[i] to image_offsets[i] + patch_counts[i] / 4 - 1; these ranges rise with i, do not intersect and lie inside the sequence; the first image starts at position 0 and the last image ends at the sequence's last position.
All inputs are finite; a program needn't handle non-finite values.
Results may differ from the reference program's by a relative error of at most 0.012.
The reference program's roundings to bfloat16 on the way (of `normed`, `merged`, `hidden`, `visual`, `normed_seq` and `weights`) count: a program that leaves them out, or rounds other values in their place, can miss the bound.
Values may be sent and summed in bfloat16 or wider, within the bound.
A program may use at most 384 MiB of HBM per device.

```python
import math
import jax
import jax.numpy as jnp
from jax import lax

D = 8192
HEAD = 128
VW = 1280
QH = 32
KVH = 4
PMAX = 1024
MW = 5120
HPD = 4
IMG = 16
LENGTH = 6144


def image_layout(key):
    base_key = jax.random.fold_in(key, 11)
    count_key, order_key, spacing_key = jax.random.split(base_key, 3)
    tokens_each = jax.random.randint(count_key, (IMG,), PMAX // 16, PMAX // 4 + 1)
    largest = jax.random.randint(order_key, (), 0, IMG - 1)
    tokens_each = tokens_each.at[largest].set(PMAX // 4).at[IMG - 1].set(PMAX // 16)
    spacing = jax.random.randint(spacing_key, (IMG - 1,), 1, 100)
    text_total = LENGTH - jnp.sum(tokens_each)
    inner_gaps = spacing * text_total // jnp.sum(spacing)
    inner_gaps = inner_gaps.at[IMG - 2].add(text_total - jnp.sum(inner_gaps))
    gaps = jnp.concatenate([jnp.zeros((1,), jnp.int32), inner_gaps.astype(jnp.int32)])
    offsets = jnp.cumsum(gaps) + jnp.cumsum(tokens_each) - tokens_each
    return ((4 * tokens_each).astype(jnp.int32), offsets.astype(jnp.int32))


def draw_patch_counts(key, part):
    return image_layout(key)[0]


def draw_image_offsets(key, part):
    return image_layout(key)[1]


def bias_values(key, length):
    values = jnp.clip(jax.random.normal(key, (length,), jnp.float32), -4.0, 4.0)
    return values.astype(jnp.bfloat16)


def draw_query_bias(key, part):
    return bias_values(jax.random.fold_in(key, 23), QH * HEAD)


def draw_key_bias(key, part):
    return bias_values(jax.random.fold_in(key, 29), KVH * HEAD)


def level_of(key, extent, cuts, low, high):
    def one(axis_at, shards_of):
        draws = jax.random.uniform(jax.random.fold_in(jax.random.fold_in(key, 6), axis_at), (shards_of,), jnp.float32, low / len(cuts), high / len(cuts))
        return jnp.repeat(jnp.exp(draws), extent[axis_at] // shards_of).reshape((-1,) + (1,) * (len(extent) - axis_at - 1))

    gain = one(*cuts[0])
    for cut in cuts[1:]:
        gain = gain * one(*cut)
    return gain


def bell_draw(own_key, shape, scale, bound, cuts=(), kind=jnp.bfloat16):
    values = jax.random.normal(own_key, shape, jnp.float32) * scale
    if len(cuts) > 0:
        values = level_of(own_key, shape, cuts, -0.22, 0.18) * values
    return jnp.clip(values, min=-bound, max=bound).astype(kind)


def setup_inputs(seed: int = 0) -> dict:
    key_of = jax.random.split(jax.random.key(seed), 18)
    patches = bell_draw(key_of[0], (IMG * PMAX, VW), 1.0, 6.0, ((0, 16),))
    norm_gain = jnp.clip(1.0 + 0.18 * jax.random.normal(key_of[1], (VW,), jnp.float32), 0.099609375, 1.8984375).astype(jnp.bfloat16)
    norm_shift = bell_draw(key_of[2], (VW,), 0.5, 3.0)
    merge_in_weight = bell_draw(key_of[3], (MW, MW), MW ** -0.5, 0.078125, ((1, 8),))
    merge_in_bias = bell_draw(key_of[4], (MW,), 0.5, 3.0, ((0, 8),))
    merge_out_weight = bell_draw(key_of[5], (MW, D), MW ** -0.5, 0.078125, ((0, 8), (1, 16)))
    merge_out_bias = bell_draw(key_of[6], (D,), 0.5, 3.0, ((0, 16),))
    text_embeds = bell_draw(key_of[7], (LENGTH, D), 1.0, 6.0, ((0, 16), (1, 4)))
    rms_gain = jnp.clip(1.0 + 0.18 * jax.random.normal(key_of[8], (D,), jnp.float32), 0.099609375, 1.8984375).astype(jnp.bfloat16)
    query_weight = bell_draw(key_of[9], (D, QH * HEAD), D ** -0.5, 0.0625, ((1, 8),))
    query_bias = draw_query_bias(jax.random.fold_in(key_of[17], 71), 0)
    key_weight = bell_draw(key_of[11], (D, KVH * HEAD), D ** -0.5, 0.0625, ((1, 4),))
    key_bias = draw_key_bias(jax.random.fold_in(key_of[17], 71), 0)
    value_weight = bell_draw(key_of[13], (D, KVH * HEAD), D ** -0.5, 0.0625, ((1, 4),))
    value_bias = bell_draw(key_of[14], (KVH * HEAD,), 0.5, 3.0, ((0, 4),))
    patch_counts = draw_patch_counts(jax.random.fold_in(key_of[17], 71), 0)
    image_offsets = draw_image_offsets(jax.random.fold_in(key_of[17], 71), 0)
    return {"patches": patches, "norm_gain": norm_gain, "norm_shift": norm_shift, "merge_in_weight": merge_in_weight, "merge_in_bias": merge_in_bias, "merge_out_weight": merge_out_weight, "merge_out_bias": merge_out_bias, "text_embeds": text_embeds, "rms_gain": rms_gain, "query_weight": query_weight, "query_bias": query_bias, "key_weight": key_weight, "key_bias": key_bias, "value_weight": value_weight, "value_bias": value_bias, "patch_counts": patch_counts, "image_offsets": image_offsets}


def layer_norm(inputs, scale_vec, shift_vec):
    values = inputs.astype(jnp.float32)
    center = values - lax.optimization_barrier(jnp.mean(values, axis=-1, keepdims=True))
    spread = lax.optimization_barrier(jnp.mean(center * center, axis=-1, keepdims=True))
    normed = center * lax.rsqrt(spread + 1e-06) * scale_vec.astype(jnp.float32) + shift_vec.astype(jnp.float32)
    return normed.astype(jnp.bfloat16)

def rms_norm(inputs, scale_vec):
    values = inputs.astype(jnp.float32)
    square_mean = lax.optimization_barrier(jnp.mean(values * values, axis=-1, keepdims=True))
    return (values * lax.rsqrt(square_mean + 1e-06) * scale_vec.astype(jnp.float32)).astype(jnp.bfloat16)

def rotate(values, positions):
    half_dim = values.shape[-1] // 2
    inv_freq = jnp.exp(jnp.arange(half_dim, dtype=jnp.float32) * (-2.0 * math.log(1000000.0) / values.shape[-1]))
    angles = positions.astype(jnp.float32)[:, None] * inv_freq[None, :]
    cosine = jnp.cos(angles)[:, None, :]
    sine_vals = jnp.sin(angles)[:, None, :]
    lower_half = values[..., :half_dim]
    upper_half = values[..., half_dim:]
    return jnp.concatenate([lower_half * cosine - upper_half * sine_vals, upper_half * cosine + lower_half * sine_vals], axis=-1)

def project(normed_seq, weight, bias_vec, positions, rotary):
    values = jnp.dot(normed_seq, weight, preferred_element_type=jnp.float32) + bias_vec.astype(jnp.float32)
    values = values.reshape(values.shape[0], -1, HEAD)
    if rotary:
        values = rotate(values, positions)
    return values.astype(jnp.bfloat16)

def visual_slots(positions, counts, offsets, per_image):
    image_start = offsets.astype(jnp.int32)
    relative = positions[:, None] - image_start[None, :]
    inside = (relative >= 0) & (relative < (counts.astype(jnp.int32) // 4)[None, :])
    images = jnp.arange(counts.shape[0], dtype=jnp.int32)
    slot_rows = lax.optimization_barrier(jnp.sum(jnp.where(inside, images[None, :] * per_image + relative, 0), axis=1)).astype(jnp.int32)
    return (slot_rows, jnp.any(inside, axis=1))

def reference(patches, norm_gain, norm_shift, merge_in_weight, merge_in_bias, merge_out_weight, merge_out_bias, text_embeds, rms_gain, query_weight, query_bias, key_weight, key_bias, value_weight, value_bias, patch_counts, image_offsets):
    per_image = PMAX // 4
    normed = layer_norm(patches, norm_gain, norm_shift)
    merged = normed.reshape(IMG * per_image, MW)
    hidden = jax.nn.gelu(jnp.dot(merged, merge_in_weight, preferred_element_type=jnp.float32) + merge_in_bias.astype(jnp.float32), approximate=False).astype(jnp.bfloat16)
    visual = (jnp.dot(hidden, merge_out_weight, preferred_element_type=jnp.float32) + merge_out_bias.astype(jnp.float32)).astype(jnp.bfloat16)
    positions = jnp.arange(LENGTH, dtype=jnp.int32)
    slot_rows, is_visual = visual_slots(positions, patch_counts, image_offsets, per_image)
    embeds = jnp.where(is_visual[:, None], jnp.take(visual, slot_rows, axis=0), text_embeds)
    normed_seq = rms_norm(embeds, rms_gain)
    queries = jnp.transpose(project(normed_seq, query_weight, query_bias, positions, True), (1, 0, 2))
    all_keys = jnp.transpose(project(normed_seq, key_weight, key_bias, positions, True), (1, 0, 2))
    all_values = jnp.transpose(project(normed_seq, value_weight, value_bias, positions, False), (1, 0, 2))
    score_scale = HEAD ** (-0.5)

    def one_head(head_idx):
        kv_group = head_idx // HPD % KVH
        scores = jnp.dot(queries[head_idx], all_keys[kv_group].T, preferred_element_type=jnp.float32) * score_scale
        scores = jnp.where(positions[None, :] <= positions[:, None], scores, -jnp.inf)
        row_max = lax.optimization_barrier(jnp.max(scores, axis=1, keepdims=True))
        exp_scores = jnp.exp(scores - row_max)
        weights = (exp_scores / lax.optimization_barrier(jnp.sum(exp_scores, axis=1, keepdims=True))).astype(jnp.bfloat16)
        return jnp.dot(weights, all_values[kv_group], preferred_element_type=jnp.float32).astype(jnp.bfloat16)
    context = lax.map(one_head, jnp.arange(QH, dtype=jnp.int32))
    context = jnp.transpose(context, (1, 0, 2)).reshape(LENGTH, QH * HEAD)
    return (embeds, context)
```

```python
import functools
import math

import jax
import jax.numpy as jnp
from jax import lax
from jax.experimental import pallas as pl
from jax.experimental.pallas import tpu as pltpu
from jax.sharding import PartitionSpec as P

HEAD = 128
MESH = pl.DeviceIdType.MESH
MIB = 1024 * 1024
ANY = pl.BlockSpec(memory_space=pl.ANY)
VMEM = pl.BlockSpec(memory_space=pltpu.VMEM)
BF16 = jnp.bfloat16
F32 = jnp.float32


def coords():
    s = lax.axis_index("section")
    q = lax.axis_index("seq")
    z = lax.div(q, 4)
    y = s * 2 + lax.rem(lax.div(q, 2), 2)
    return z, y, lax.rem(q, 2), lax.axis_index("mp")


def place(z, y, c):
    return lax.div(y, 2), z * 4 + lax.rem(y, 2) * 2 + c


def device(z, y, c, x):
    s, q = place(z, y, c)
    return {"section": s, "seq": q, "mp": x}


def merge_in_kernel(x_ref, gain_ref, shift_ref, w_ref, b_ref, o_ref, normed, joined):
    width = x_ref.shape[1]
    rows = x_ref.shape[0] // 4
    tiles = width // 128

    @pl.when(pl.program_id(0) == 0)
    def _():
        def body(i, carry):
            block = pl.ds(pl.multiple_of(i * 64, 64), 64)
            values = x_ref[block, :].astype(F32)
            center = values - jnp.mean(values, axis=-1, keepdims=True)
            spread = jnp.mean(center * center, axis=-1, keepdims=True)
            result = center * lax.rsqrt(spread + 1e-06) * gain_ref[...] + shift_ref[...]
            for u in range(tiles):
                normed[u, block, :] = result[:, u * 128 : (u + 1) * 128]
            return carry

        lax.fori_loop(0, x_ref.shape[0] // 64, body, 0)
        for t in range(4):
            for u in range(tiles):
                cols = slice((t * tiles + u) * 128, (t * tiles + u + 1) * 128)
                joined[:, cols] = normed[u, pl.ds(t, rows, stride=4), :].astype(BF16)

    total = jnp.dot(joined[...], w_ref[...], preferred_element_type=F32) + b_ref[...]
    o_ref[...] = (0.5 * total * (1.0 + lax.erf(total * (2.0**-0.5)))).astype(BF16)


def merge_in(patches, gain, shift, weight, bias):
    rows, width = patches.shape
    cols = weight.shape[1]
    step = 128
    return pl.pallas_call(
        merge_in_kernel,
        grid=(cols // step,),
        in_specs=[
            pl.BlockSpec((rows, width), lambda i: (0, 0)),
            pl.BlockSpec((1, width), lambda i: (0, 0)),
            pl.BlockSpec((1, width), lambda i: (0, 0)),
            pl.BlockSpec((4 * width, step), lambda i: (0, i)),
            pl.BlockSpec((1, step), lambda i: (0, i)),
        ],
        out_specs=pl.BlockSpec((rows // 4, step), lambda i: (0, i)),
        out_shape=jax.ShapeDtypeStruct((rows // 4, cols), BF16),
        scratch_shapes=[
            pltpu.VMEM((width // 128, rows, 128), F32),
            pltpu.VMEM((rows // 4, 4 * width), BF16),
        ],
        compiler_params=pltpu.CompilerParams(vmem_limit_bytes=40 * MIB),
        name="merge_in",
    )(
        patches,
        gain.astype(F32)[None, :],
        shift.astype(F32)[None, :],
        weight,
        bias.astype(F32)[None, :],
    )


def torus_gather_kernel(extra, x_ref, *refs):
    n_in = extra.n_in if extra else 0
    n_out = extra.n_out if extra else 0
    extra_in = refs[:n_in]
    out_ref = refs[n_in]
    extra_out = refs[n_in + 1 : n_in + 1 + n_out]
    a_send, a_recv, b_send, b_recv, s_send, s_recv, own_sem = refs[n_in + 1 + n_out : n_in + 8 + n_out]
    extra_sems = refs[n_in + 8 + n_out :]
    z, y, c, x = coords()
    half = x_ref.shape[0] // 2

    def chip(da, db, core):
        zz = lax.rem(z + da * (1 - core) + db * core + 8, 4)
        yy = lax.rem(y + da * core + db * (1 - core) + 8, 4)
        return zz, yy

    def where(da, db, core):
        zz, yy = chip(da, db, core)
        return place(zz, yy, core)

    def target(da, db):
        zz, yy = chip(da, db, c)
        return device(zz, yy, c, x)

    sibling = device(z, y, 1 - c, x)
    barrier = pltpu.get_barrier_semaphore()
    peers = [target(1, 0), target(-1, 0), target(0, 1), target(0, -1), sibling]
    if extra:
        peers = peers + extra.peers(z, y, c, x)
    for peer in peers:
        pl.semaphore_signal(barrier, inc=1, device_id=peer, device_id_type=MESH)
    pl.semaphore_wait(barrier, len(peers))

    started = []

    def view(da, db, core, part):
        s, q = where(da, db, core)
        if part is None:
            return out_ref.at[s, q]
        return out_ref.at[s, q, pl.ds(part * half, half)]

    def send(da, db, part, send_sem, recv_sem, to):
        source = view(da, db, c, part)
        if da == 0 and db == 0:
            source = x_ref
        copy = pltpu.make_async_remote_copy(
            src_ref=source,
            dst_ref=view(da, db, c, part),
            send_sem=send_sem,
            recv_sem=recv_sem,
            device_id=to,
            device_id_type=MESH,
        )
        copy.start()
        started.append(copy)

    def arrived(da, db, core, part, recv_sem, send_sem):
        block = view(da, db, core, part)
        pltpu.make_async_remote_copy(
            src_ref=block,
            dst_ref=block,
            send_sem=send_sem,
            recv_sem=recv_sem,
            device_id=sibling,
            device_id_type=MESH,
        ).wait_recv()

    def along_b(a, da):
        send(da, 0, None, b_send.at[a, 0], b_recv.at[a, 0], target(0, 1))
        send(da, 0, None, b_send.at[a, 1], b_recv.at[a, 1], target(0, -1))
        send(da, 0, None, s_send.at[a, 0], s_recv.at[a, 0], sibling)

    offsets = [0, -1, 1, 2]
    send(0, 0, None, a_send.at[0], a_recv.at[0], target(1, 0))
    send(0, 0, None, a_send.at[1], a_recv.at[1], target(-1, 0))
    along_b(0, 0)
    own_copy = pltpu.make_async_copy(x_ref, view(0, 0, c, None), own_sem)
    own_copy.start()
    if extra:
        extra_wait = extra.start(z, y, c, x, extra_in, extra_out, extra_sems)

    arrived(-1, 0, c, None, a_recv.at[0], a_send.at[0])
    send(-1, 0, 0, a_send.at[2], a_recv.at[2], target(1, 0))
    along_b(1, -1)
    arrived(1, 0, c, None, a_recv.at[1], a_send.at[1])
    send(1, 0, 1, a_send.at[3], a_recv.at[3], target(-1, 0))
    along_b(2, 1)

    def relay_b(a):
        da = offsets[a]
        arrived(da, -1, c, None, b_recv.at[a, 0], b_send.at[a, 0])
        send(da, -1, 0, b_send.at[a, 2], b_recv.at[a, 2], target(0, 1))
        send(da, -1, None, s_send.at[a, 1], s_recv.at[a, 1], sibling)
        arrived(da, 1, c, None, b_recv.at[a, 1], b_send.at[a, 1])
        send(da, 1, 1, b_send.at[a, 3], b_recv.at[a, 3], target(0, -1))
        send(da, 1, None, s_send.at[a, 2], s_recv.at[a, 2], sibling)

    relay_b(0)
    arrived(2, 0, c, 0, a_recv.at[2], a_send.at[2])
    arrived(2, 0, c, 1, a_recv.at[3], a_send.at[3])
    along_b(3, 2)
    for a in (1, 2, 3):
        relay_b(a)
    for a in range(4):
        da = offsets[a]
        arrived(da, 2, c, 0, b_recv.at[a, 2], b_send.at[a, 2])
        arrived(da, 2, c, 1, b_recv.at[a, 3], b_send.at[a, 3])
        send(da, 2, None, s_send.at[a, 3], s_recv.at[a, 3], sibling)
    for a in range(4):
        for b in range(4):
            arrived(offsets[a], offsets[b], 1 - c, None, s_recv.at[a, b], s_send.at[a, b])
    own_copy.wait()
    for copy in started:
        copy.wait_send()
    if extra:
        extra_wait()


def torus_gather(shard, collective_id, name, extra=None, operands=()):
    rows, cols = shard.shape
    dma = pltpu.SemaphoreType.DMA
    outs = [jax.ShapeDtypeStruct((2, 16, rows, cols), shard.dtype)]
    sems = [dma((4,)), dma((4,)), dma((4, 4)), dma((4, 4)), dma((4, 4)), dma((4, 4)), dma]
    if extra:
        outs = outs + extra.out_shapes
        sems = sems + extra.sems
    return pl.pallas_call(
        functools.partial(torus_gather_kernel, extra),
        out_shape=outs,
        in_specs=[ANY] * (1 + len(operands)),
        out_specs=[ANY] * len(outs),
        scratch_shapes=sems,
        compiler_params=pltpu.CompilerParams(collective_id=collective_id, has_side_effects=True),
        name=name,
    )(shard, *operands)


class Early:
    n_in = 2
    n_out = 2
    out_shapes = [
        jax.ShapeDtypeStruct((4, 96, 2048), BF16),
        jax.ShapeDtypeStruct((2, 640, 256), BF16),
    ]
    sems = [
        pltpu.SemaphoreType.DMA((4,)),
        pltpu.SemaphoreType.DMA((4,)),
        pltpu.SemaphoreType.DMA((2,)),
        pltpu.SemaphoreType.DMA((2,)),
    ]

    @staticmethod
    def peers(z, y, c, x):
        across = [device(z, y, c, lax.rem(x + d, 4)) for d in (1, 2, 3)]
        return across + [device(z, lax.rem(y + 2, 4), c, x)]

    @staticmethod
    def start(z, y, c, x, ins, outs, sems):
        text, weight = ins
        rows_out, weight_out = outs
        t_send, t_recv, w_send, w_recv = sems
        s = lax.div(y, 2)
        copies = []
        for d in (1, 2, 3):
            to = lax.rem(x + d, 4)
            copies.append(
                pltpu.make_async_remote_copy(
                    src_ref=text.at[pl.ds(pl.multiple_of(to * 96, 96), 96)],
                    dst_ref=rows_out.at[x],
                    send_sem=t_send.at[d],
                    recv_sem=t_recv.at[d],
                    device_id=device(z, y, c, to),
                    device_id_type=MESH,
                )
            )
        other = 1 - s
        copies.append(
            pltpu.make_async_remote_copy(
                src_ref=weight.at[:, pl.ds(pl.multiple_of(other * 256, 256), 256)],
                dst_ref=weight_out.at[s],
                send_sem=w_send.at[0],
                recv_sem=w_recv.at[0],
                device_id=device(z, lax.rem(y + 2, 4), c, x),
                device_id_type=MESH,
            )
        )
        copies.append(
            pltpu.make_async_copy(
                text.at[pl.ds(pl.multiple_of(x * 96, 96), 96)], rows_out.at[x], t_send.at[0]
            )
        )
        copies.append(
            pltpu.make_async_copy(
                weight.at[:, pl.ds(pl.multiple_of(s * 256, 256), 256)], weight_out.at[s], w_send.at[1]
            )
        )
        for copy in copies:
            copy.start()

        def wait():
            for d in (1, 2, 3):
                source = lax.rem(x + 4 - d, 4)
                pltpu.make_async_remote_copy(
                    src_ref=rows_out.at[source],
                    dst_ref=rows_out.at[source],
                    send_sem=t_send.at[d],
                    recv_sem=t_recv.at[d],
                    device_id=device(z, y, c, source),
                    device_id_type=MESH,
                ).wait_recv()
                copies[d - 1].wait_send()
            pltpu.make_async_remote_copy(
                src_ref=weight_out.at[other],
                dst_ref=weight_out.at[other],
                send_sem=w_send.at[0],
                recv_sem=w_recv.at[0],
                device_id=device(z, lax.rem(y + 2, 4), c, x),
                device_id_type=MESH,
            ).wait_recv()
            copies[3].wait_send()
            copies[4].wait()
            copies[5].wait()

        return wait


GROUP = 32


def merge_out_kernel(start_a, start_b, begin_b, h_ref, w_ref, o_ref, product):
    i = pl.program_id(0)
    total = jnp.dot(h_ref[0, 0], w_ref[0], preferred_element_type=F32)
    total = total + jnp.dot(h_ref[1, 0], w_ref[1], preferred_element_type=F32)
    for half in range(2):
        product[half, pl.ds(pl.multiple_of(i * 256, 256), 256), :] = total[:, half * 128 : (half + 1) * 128]

    @pl.when(i == pl.num_programs(0) - 1)
    def _():
        row = lax.broadcasted_iota(jnp.int32, (GROUP, 128), 0)

        def body(q, carry):
            for m in range(4):
                for k in range(3):
                    g = q * 12 + m * 3 + k
                    for half in range(2):
                        first = product[half, pl.ds(start_a[g], GROUP), :]
                        second = product[half, pl.ds(start_b[g], GROUP), :]
                        chosen = jnp.where(row >= begin_b[g], second, first).astype(BF16)
                        o_ref[m, k, q, :, half * 128 : (half + 1) * 128] = chosen
            return carry

        lax.fori_loop(0, 16, body, 0)


def merge_out(hidden, weight, start_a, start_b, begin_b):
    return pl.pallas_call(
        merge_out_kernel,
        grid_spec=pltpu.PrefetchScalarGridSpec(
            num_scalar_prefetch=3,
            grid=(16,),
            in_specs=[
                pl.BlockSpec((2, 1, 256, 640), lambda i, *_: (0, i, 0, 0)),
                pl.BlockSpec((2, 640, 256), lambda i, *_: (0, 0, 0)),
            ],
            out_specs=pl.BlockSpec((4, 3, 16, GROUP, 256), lambda i, *_: (0, 0, 0, 0, 0)),
            scratch_shapes=[pltpu.VMEM((2, 4096 + GROUP, 128), F32)],
        ),
        out_shape=jax.ShapeDtypeStruct((4, 3, 16, GROUP, 256), BF16),
        compiler_params=pltpu.CompilerParams(vmem_limit_bytes=40 * MIB),
        name="merge_out",
    )(start_a, start_b, begin_b, hidden, weight)


def spread_kernel(part, bias, text, visual_mask, out, summed, got, rows, r_send, r_recv, v_send, v_recv, own_sem, g_send, g_recv):
    z, y, c, x = coords()
    s, q = place(z, y, c)
    linear = s * 16 + q
    barrier = pltpu.get_barrier_semaphore()

    def peer(j):
        other = lax.rem(linear + j, 32)
        return lax.div(other, 16), lax.rem(other, 16)

    for d in (1, 2, 3):
        pl.semaphore_signal(
            barrier, inc=1, device_id=device(z, y, c, lax.rem(x + d, 4)), device_id_type=MESH
        )

    def greet(j, carry):
        ps, pq = peer(j)
        pl.semaphore_signal(
            barrier, inc=1, device_id={"section": ps, "seq": pq, "mp": x}, device_id_type=MESH
        )
        return carry

    lax.fori_loop(1, 32, greet, 0)
    pl.semaphore_wait(barrier, 34)

    def sum_copy(k, d):
        to = lax.rem(x + d, 4)
        return pltpu.make_async_remote_copy(
            src_ref=part.at[to, k],
            dst_ref=got.at[k, d - 1],
            send_sem=r_send.at[k, d - 1],
            recv_sem=r_recv.at[k, d - 1],
            device_id=device(z, y, c, to),
            device_id_type=MESH,
        )

    def start_sums(k):
        for d in (2, 1, 3):
            sum_copy(k, d).start()

    def add_up(k):
        for d in (1, 2, 3):
            sum_copy(k, d).wait_recv()

        def body(i, carry):
            total = part[x, k, i].astype(F32) + bias[...]
            for d in range(3):
                total = total + got[k, d, i].astype(F32)
            summed[k, i] = total.astype(BF16)
            return carry

        lax.fori_loop(0, 16, body, 0)

    def owner_copy(k, j):
        ps, pq = peer(j)
        return pltpu.make_async_remote_copy(
            src_ref=summed.at[k, pq],
            dst_ref=rows.at[k, q * 2 + s],
            send_sem=v_send.at[k],
            recv_sem=v_recv.at[k],
            device_id={"section": ps, "seq": pq, "mp": x},
            device_id_type=MESH,
        )

    def start_owner(k):
        def body(j, carry):
            owner_copy(k, j).start()
            return carry

        lax.fori_loop(1, 32, body, 0)
        pltpu.make_async_copy(summed.at[k, q], rows.at[k, q * 2 + s], own_sem.at[k]).start()

    def place_rows(k):
        pltpu.make_async_copy(summed.at[k, q], rows.at[k, q * 2 + s], own_sem.at[k]).wait()
        pltpu.make_async_copy(rows.at[k, pl.ds(0, 31)], rows.at[k, pl.ds(0, 31)], v_recv.at[k]).wait()
        visual = visual_mask[k * 32 : (k + 1) * 32, :] > 0.5
        for b in range(32):
            own_text = text[b // 8, k * 32 : (k + 1) * 32, (b % 8) * 256 : (b % 8 + 1) * 256]
            out[k, x, b] = jnp.where(visual, rows[k, b].astype(F32), own_text.astype(F32)).astype(BF16)

    def row_copy(k, part_index, origin, to, slot):
        if part_index is None:
            block = out.at[k, origin]
        else:
            block = out.at[k, origin, pl.ds(part_index * 16, 16)]
        return pltpu.make_async_remote_copy(
            src_ref=block,
            dst_ref=block,
            send_sem=g_send.at[k, slot],
            recv_sem=g_recv.at[k, slot],
            device_id=device(z, y, c, to),
            device_id_type=MESH,
        )

    right, left, across = lax.rem(x + 1, 4), lax.rem(x + 3, 4), lax.rem(x + 2, 4)

    def start_rows(k):
        row_copy(k, None, x, right, 0).start()
        row_copy(k, None, x, left, 1).start()

    def relay_rows(k):
        row_copy(k, None, left, right, 0).wait_recv()
        row_copy(k, 0, left, right, 2).start()
        row_copy(k, None, right, left, 1).wait_recv()
        row_copy(k, 1, right, left, 3).start()

    start_sums(0)
    start_sums(1)
    add_up(0)
    start_owner(0)
    start_sums(2)
    add_up(1)
    start_owner(1)
    place_rows(0)
    start_rows(0)
    add_up(2)
    start_owner(2)
    relay_rows(0)
    place_rows(1)
    start_rows(1)
    place_rows(2)
    start_rows(2)
    relay_rows(1)
    relay_rows(2)
    for k in range(3):
        row_copy(k, 0, across, right, 2).wait_recv()
        row_copy(k, 1, across, left, 3).wait_recv()
    for k in range(3):
        for d in (1, 2, 3):
            sum_copy(k, d).wait_send()
        pltpu.make_async_copy(rows.at[k, pl.ds(0, 31)], rows.at[k, pl.ds(0, 31)], v_send.at[k]).wait()
        row_copy(k, None, x, right, 0).wait_send()
        row_copy(k, None, x, left, 1).wait_send()
        row_copy(k, 0, left, right, 2).wait_send()
        row_copy(k, 1, right, left, 3).wait_send()


def spread(part, bias, text, visual_mask):
    dma = pltpu.SemaphoreType.DMA
    return pl.pallas_call(
        spread_kernel,
        out_shape=jax.ShapeDtypeStruct((3, 4, 32, GROUP, 256), BF16),
        in_specs=[VMEM] * 4,
        out_specs=VMEM,
        scratch_shapes=[
            pltpu.VMEM((3, 16, GROUP, 256), BF16),
            pltpu.VMEM((3, 3, 16, GROUP, 256), BF16),
            pltpu.VMEM((3, 32, GROUP, 256), BF16),
            dma((3, 3)),
            dma((3, 3)),
            dma((3,)),
            dma((3,)),
            dma((3,)),
            dma((3, 4)),
            dma((3, 4)),
        ],
        compiler_params=pltpu.CompilerParams(
            collective_id=2, has_side_effects=True, vmem_limit_bytes=48 * MIB
        ),
        name="spread",
    )(part, bias, text, visual_mask)


def project_kernel(x_ref, gain_ref, wq, wk, wv, bias, cos_ref, sin_ref, q_out, k_out, v_out, e_out, scale, total):
    i = pl.program_id(0)
    blocks = wq.shape[0] // 256
    order = [(k, m) for m in range(4) for k in range(3)]

    def rows_of(b):
        return jnp.concatenate([x_ref[k, m, b] for k, m in order], axis=0)

    @pl.when(i == 0)
    def _():
        def body(b, carry):
            values = rows_of(b).astype(F32)
            return carry + values * values

        squares = lax.fori_loop(0, 32, body, jnp.zeros((384, 256), F32))
        mean = jnp.sum(squares, axis=-1, keepdims=True) * (1.0 / 8192.0)
        scale[...] = jnp.broadcast_to(lax.rsqrt(mean + 1e-06), (384, 256))
        total[...] = jnp.broadcast_to(bias[...], total.shape)
        m0 = lax.axis_index("mp")
        for j in range(8):
            e_out[:, j * 256 : (j + 1) * 256] = rows_of(m0 * 8 + j)

    for j in range(blocks):
        b = i * blocks + j
        normed = (rows_of(b).astype(F32) * scale[...] * gain_ref[b]).astype(BF16)
        span = slice(j * 256, (j + 1) * 256)
        total[:, :512] += jnp.dot(normed, wq[span, :], preferred_element_type=F32)
        both = jnp.concatenate([wk[span, :], wv[span, :]], axis=1)
        total[:, 512:] += jnp.dot(normed, both, preferred_element_type=F32)

    @pl.when(i == pl.num_programs(0) - 1)
    def _():
        def rotate(values):
            return values * cos_ref[...] + pltpu.roll(values, 64, 1) * sin_ref[...]

        for h in range(4):
            cols = slice(h * 128, (h + 1) * 128)
            q_out[:, cols] = rotate(total[:, cols]).astype(BF16)
        k_out[...] = rotate(total[:, 512:640]).astype(BF16)
        v_out[...] = total[:, 640:].astype(BF16)


def project(x, gain, wq, wk, wv, bias, cos, sin):
    depth = 1024
    whole = lambda shape: pl.BlockSpec(shape, lambda i: (0,) * len(shape))
    return pl.pallas_call(
        project_kernel,
        grid=(8192 // depth,),
        in_specs=[
            whole(x.shape),
            whole((32, 1, 256)),
            pl.BlockSpec((depth, 512), lambda i: (i, 0)),
            pl.BlockSpec((depth, 128), lambda i: (i, 0)),
            pl.BlockSpec((depth, 128), lambda i: (i, 0)),
            whole((1, 768)),
            whole((384, 128)),
            whole((384, 128)),
        ],
        out_specs=[whole((384, 512)), whole((384, 128)), whole((384, 128)), whole((384, 2048))],
        out_shape=[
            jax.ShapeDtypeStruct((384, 512), BF16),
            jax.ShapeDtypeStruct((384, 128), BF16),
            jax.ShapeDtypeStruct((384, 128), BF16),
            jax.ShapeDtypeStruct((384, 2048), BF16),
        ],
        scratch_shapes=[pltpu.VMEM((384, 256), F32), pltpu.VMEM((384, 768), F32)],
        compiler_params=pltpu.CompilerParams(vmem_limit_bytes=48 * MIB),
        name="project",
    )(x, gain, wq, wk, wv, bias, cos, sin)


def attention_kernel(q_ref, kv_ref, o_ref, peak, norm, total):
    own = lax.axis_index("seq")
    rows = q_ref.shape[0]
    factor = HEAD**-0.5 * math.log2(math.e)
    peak[...] = jnp.full(peak.shape, -jnp.inf, F32)
    norm[...] = jnp.zeros(norm.shape, F32)
    total[...] = jnp.zeros(total.shape, F32)

    def block(j, masked):
        keys = kv_ref[0, j]
        values = kv_ref[1, j]
        for h in range(4):
            query = q_ref[:, h * HEAD : (h + 1) * HEAD]
            scores = lax.dot_general(
                query, keys, (((1,), (1,)), ((), ())), preferred_element_type=F32
            )
            if masked:
                row = lax.broadcasted_iota(jnp.int32, scores.shape, 0)
                col = lax.broadcasted_iota(jnp.int32, scores.shape, 1)
                scores = jnp.where(col <= row, scores, -jnp.inf)
            before = peak[h]
            after = jnp.maximum(before, jnp.max(scores, axis=1, keepdims=True))
            weights = jnp.exp2((scores - after[:, :1]) * factor)
            fade = jnp.exp2((before - after) * factor)
            peak[h] = after
            norm[h] = norm[h] * fade + jnp.sum(weights, axis=1, keepdims=True)
            total[h] = total[h] * fade + jnp.dot(
                weights.astype(BF16), values, preferred_element_type=F32
            )

    block(own, True)

    def body(j, carry):
        block(j, False)
        return carry

    lax.fori_loop(0, own, body, 0)
    for h in range(4):
        o_ref[:, h * HEAD : (h + 1) * HEAD] = (total[h] / norm[h]).astype(BF16)


def attention(queries, keys_values):
    rows = queries.shape[0]
    return pl.pallas_call(
        attention_kernel,
        out_shape=jax.ShapeDtypeStruct(queries.shape, BF16),
        in_specs=[VMEM, VMEM],
        out_specs=VMEM,
        scratch_shapes=[pltpu.VMEM((4, rows, HEAD), F32)] * 3,
        compiler_params=pltpu.CompilerParams(vmem_limit_bytes=40 * MIB),
        name="attention",
    )(queries, keys_values)


def local(
    patches,
    norm_gain,
    norm_shift,
    merge_in_weight,
    merge_in_bias,
    merge_out_weight,
    merge_out_bias,
    text_embeds,
    rms_gain,
    query_weight,
    query_bias,
    key_weight,
    key_bias,
    value_weight,
    value_bias,
    patch_counts,
    image_offsets,
):
    section = lax.axis_index("section")
    seq = lax.axis_index("seq")
    col = lax.axis_index("mp")
    own_rows = text_embeds.shape[0]
    tokens = patch_counts // 4
    first = jnp.arange(6144 // GROUP, dtype=jnp.int32) * GROUP
    image_a = jnp.sum((image_offsets[None, :] <= first[:, None]).astype(jnp.int32), axis=1) - 1
    image_b = jnp.minimum(image_a + 1, 15)
    pick_a = image_a[:, None] == jnp.arange(16, dtype=jnp.int32)[None, :]
    pick_b = image_b[:, None] == jnp.arange(16, dtype=jnp.int32)[None, :]
    offset_a = jnp.sum(jnp.where(pick_a, image_offsets[None, :], 0), axis=1)
    offset_b = jnp.sum(jnp.where(pick_b, image_offsets[None, :], 0), axis=1)
    begin_b = jnp.where(image_a == 15, GROUP, jnp.minimum(offset_b - first, GROUP))
    start_a = jnp.minimum(image_a * 256 + first - offset_a, 4096)
    start_b = image_b * 256 - begin_b
    own_positions = seq * own_rows + jnp.arange(own_rows, dtype=jnp.int32)
    block_positions = seq * own_rows + col * 96 + jnp.arange(96, dtype=jnp.int32)
    relative = block_positions[:, None] - image_offsets[None, :]
    is_visual = jnp.any((relative >= 0) & (relative < tokens[None, :]), axis=1)
    visual_mask = jnp.broadcast_to(is_visual[:, None].astype(F32), (96, 256))
    half_dim = HEAD // 2
    inv_freq = jnp.exp(jnp.arange(half_dim, dtype=F32) * (-2.0 * math.log(1000000.0) / HEAD))
    angles = own_positions.astype(F32)[:, None] * inv_freq[None, :]
    cosine, sine = jnp.cos(angles), jnp.sin(angles)
    cos_table = jnp.concatenate([cosine, cosine], axis=1)
    sin_table = jnp.concatenate([-sine, sine], axis=1)

    hidden = merge_in(patches, norm_gain, norm_shift, merge_in_weight, merge_in_bias)
    all_hidden, text_rows, out_weight = torus_gather(
        hidden, 0, "gather_hidden", Early, (text_embeds, merge_out_weight)
    )
    part = merge_out(all_hidden, out_weight, start_a, start_b, begin_b)
    out_bias = lax.dynamic_slice_in_dim(merge_out_bias, section * 256, 256, 0).astype(F32)[None, :]
    rows = spread(part, out_bias, text_rows, visual_mask)
    bias = jnp.concatenate([query_bias, key_bias, value_bias]).astype(F32)[None, :]
    gain = rms_gain.astype(F32).reshape(32, 1, 256)
    queries, keys, values, embeds = project(
        rows, gain, query_weight, key_weight, value_weight, bias, cos_table, sin_table
    )
    shared = jnp.where(section == 0, keys, values)
    (keys_values,) = torus_gather(shared, 1, "gather_keys")
    return (embeds, attention(queries, keys_values))


def solution(mesh):
    placed = (
        P("seq", None),
        P(),
        P(),
        P(None, ("section", "mp")),
        P(("section", "mp")),
        P(("section", "mp"), "seq"),
        P("seq"),
        P("seq", "mp"),
        P(),
        P(None, ("section", "mp")),
        P(("section", "mp")),
        P(None, "mp"),
        P("mp"),
        P(None, "mp"),
        P("mp"),
        P(),
        P(),
    )
    return jax.shard_map(
        local,
        mesh=mesh,
        in_specs=placed,
        out_specs=(P("seq", "mp"), P("seq", ("section", "mp"))),
        check_vma=False,
    )
```

```python
import math

import jax
import jax.numpy as jnp
from jax import lax
from jax.experimental import pallas as pl
from jax.experimental.pallas import tpu as pltpu
from jax.sharding import PartitionSpec as P

HEAD = 128
MESH = pl.DeviceIdType.MESH
MIB = 1024 * 1024
ANY = pl.BlockSpec(memory_space=pl.ANY)
VMEM = pl.BlockSpec(memory_space=pltpu.VMEM)
BF16 = jnp.bfloat16
F32 = jnp.float32


def coords():
    s = lax.axis_index("section")
    q = lax.axis_index("seq")
    z = lax.div(q, 4)
    y = s * 2 + lax.rem(lax.div(q, 2), 2)
    return z, y, lax.rem(q, 2), lax.axis_index("mp")


def place(z, y, c):
    return lax.div(y, 2), z * 4 + lax.rem(y, 2) * 2 + c


def device(z, y, c, x):
    s, q = place(z, y, c)
    return {"section": s, "seq": q, "mp": x}


def merge_in_kernel(x_ref, gain_ref, shift_ref, w_ref, b_ref, o_ref, normed, joined):
    width = x_ref.shape[1]
    rows = x_ref.shape[0] // 4
    tiles = width // 128

    @pl.when(pl.program_id(0) == 0)
    def _():
        def body(i, carry):
            block = pl.ds(pl.multiple_of(i * 64, 64), 64)
            values = x_ref[block, :].astype(F32)
            center = values - jnp.mean(values, axis=-1, keepdims=True)
            spread = jnp.mean(center * center, axis=-1, keepdims=True)
            result = center * lax.rsqrt(spread + 1e-06) * gain_ref[...] + shift_ref[...]
            for u in range(tiles):
                normed[u, block, :] = result[:, u * 128 : (u + 1) * 128]
            return carry

        lax.fori_loop(0, x_ref.shape[0] // 64, body, 0)
        for t in range(4):
            for u in range(tiles):
                cols = slice((t * tiles + u) * 128, (t * tiles + u + 1) * 128)
                joined[:, cols] = normed[u, pl.ds(t, rows, stride=4), :].astype(BF16)

    total = jnp.dot(joined[...], w_ref[...], preferred_element_type=F32) + b_ref[...]
    o_ref[...] = (0.5 * total * (1.0 + lax.erf(total * (2.0**-0.5)))).astype(BF16)


def merge_in(patches, gain, shift, weight, bias):
    rows, width = patches.shape
    cols = weight.shape[1]
    step = 128
    return pl.pallas_call(
        merge_in_kernel,
        grid=(cols // step,),
        in_specs=[
            pl.BlockSpec((rows, width), lambda i: (0, 0)),
            pl.BlockSpec((1, width), lambda i: (0, 0)),
            pl.BlockSpec((1, width), lambda i: (0, 0)),
            pl.BlockSpec((4 * width, step), lambda i: (0, i)),
            pl.BlockSpec((1, step), lambda i: (0, i)),
        ],
        out_specs=pl.BlockSpec((rows // 4, step), lambda i: (0, i)),
        out_shape=jax.ShapeDtypeStruct((rows // 4, cols), BF16),
        scratch_shapes=[
            pltpu.VMEM((width // 128, rows, 128), F32),
            pltpu.VMEM((rows // 4, 4 * width), BF16),
        ],
        compiler_params=pltpu.CompilerParams(vmem_limit_bytes=60 * MIB),
        name="merge_in",
    )(
        patches,
        gain.astype(F32)[None, :],
        shift.astype(F32)[None, :],
        weight,
        bias.astype(F32)[None, :],
    )


def torus_sems():
    dma = pltpu.SemaphoreType.DMA
    return [dma((4,)), dma((4,)), dma((4, 4)), dma((4, 4)), dma((4, 4)), dma((4, 4)), dma]


class Torus:
    def __init__(self, x_ref, out_ref, sems):
        self.x_ref, self.out_ref = x_ref, out_ref
        self.a_send, self.a_recv, self.b_send, self.b_recv, self.s_send, self.s_recv, self.own_sem = sems
        self.z, self.y, self.c, self.x = coords()
        self.half = x_ref.shape[0] // 2
        self.started = []
        self.sibling = device(self.z, self.y, 1 - self.c, self.x)

    def where(self, da, db, core):
        zz = lax.rem(self.z + da * (1 - core) + db * core + 8, 4)
        yy = lax.rem(self.y + da * core + db * (1 - core) + 8, 4)
        return place(zz, yy, core)

    def target(self, da, db):
        s, q = self.where(da, db, self.c)
        return {"section": s, "seq": q, "mp": self.x}

    def peers(self):
        return [self.target(1, 0), self.target(-1, 0), self.target(0, 1), self.target(0, -1), self.sibling]

    def view(self, da, db, core, part):
        s, q = self.where(da, db, core)
        if part is None:
            return self.out_ref.at[s, q]
        return self.out_ref.at[s, q, pl.ds(part * self.half, self.half)]

    def send(self, da, db, part, send_sem, recv_sem, to):
        block = self.view(da, db, self.c, part)
        copy = pltpu.make_async_remote_copy(
            src_ref=self.x_ref if da == 0 and db == 0 else block,
            dst_ref=block,
            send_sem=send_sem,
            recv_sem=recv_sem,
            device_id=to,
            device_id_type=MESH,
        )
        copy.start()
        self.started.append(copy)

    def arrived(self, da, db, core, part, send_sem, recv_sem):
        block = self.view(da, db, core, part)
        pltpu.make_async_remote_copy(
            src_ref=block,
            dst_ref=block,
            send_sem=send_sem,
            recv_sem=recv_sem,
            device_id=self.sibling,
            device_id_type=MESH,
        ).wait_recv()

    def along_b(self, a, da):
        self.send(da, 0, None, self.b_send.at[a, 0], self.b_recv.at[a, 0], self.target(0, 1))
        self.send(da, 0, None, self.b_send.at[a, 1], self.b_recv.at[a, 1], self.target(0, -1))
        self.send(da, 0, None, self.s_send.at[a, 0], self.s_recv.at[a, 0], self.sibling)

    def start(self):
        self.send(0, 0, None, self.a_send.at[0], self.a_recv.at[0], self.target(1, 0))
        self.send(0, 0, None, self.a_send.at[1], self.a_recv.at[1], self.target(-1, 0))
        self.along_b(0, 0)
        self.own_copy = pltpu.make_async_copy(self.x_ref, self.view(0, 0, self.c, None), self.own_sem)
        self.own_copy.start()

    def run(self, use):
        offsets = [0, -1, 1, 2]
        c = self.c

        def from_sibling(a, b):
            da, db = offsets[a], offsets[b]
            self.arrived(da, db, 1 - c, None, self.s_send.at[a, b], self.s_recv.at[a, b])
            use(*self.where(da, db, 1 - c))

        def relay_b(a):
            da = offsets[a]
            self.arrived(da, -1, c, None, self.b_send.at[a, 0], self.b_recv.at[a, 0])
            self.send(da, -1, 0, self.b_send.at[a, 2], self.b_recv.at[a, 2], self.target(0, 1))
            self.send(da, -1, None, self.s_send.at[a, 1], self.s_recv.at[a, 1], self.sibling)
            self.arrived(da, 1, c, None, self.b_send.at[a, 1], self.b_recv.at[a, 1])
            self.send(da, 1, 1, self.b_send.at[a, 3], self.b_recv.at[a, 3], self.target(0, -1))
            self.send(da, 1, None, self.s_send.at[a, 2], self.s_recv.at[a, 2], self.sibling)
            use(*self.where(da, -1, c))
            use(*self.where(da, 1, c))

        self.own_copy.wait()
        use(*self.where(0, 0, c))
        self.arrived(-1, 0, c, None, self.a_send.at[0], self.a_recv.at[0])
        self.send(-1, 0, 0, self.a_send.at[2], self.a_recv.at[2], self.target(1, 0))
        self.along_b(1, -1)
        self.arrived(1, 0, c, None, self.a_send.at[1], self.a_recv.at[1])
        self.send(1, 0, 1, self.a_send.at[3], self.a_recv.at[3], self.target(-1, 0))
        self.along_b(2, 1)
        use(*self.where(-1, 0, c))
        use(*self.where(1, 0, c))
        from_sibling(0, 0)
        relay_b(0)
        self.arrived(2, 0, c, 0, self.a_send.at[2], self.a_recv.at[2])
        self.arrived(2, 0, c, 1, self.a_send.at[3], self.a_recv.at[3])
        self.along_b(3, 2)
        use(*self.where(2, 0, c))
        from_sibling(1, 0)
        from_sibling(2, 0)
        for a in (1, 2, 3):
            relay_b(a)
            from_sibling(a - 1, 1)
            from_sibling(a - 1, 2)
        from_sibling(3, 0)
        from_sibling(3, 1)
        from_sibling(3, 2)
        for a in range(4):
            da = offsets[a]
            self.arrived(da, 2, c, 0, self.b_send.at[a, 2], self.b_recv.at[a, 2])
            self.arrived(da, 2, c, 1, self.b_send.at[a, 3], self.b_recv.at[a, 3])
            self.send(da, 2, None, self.s_send.at[a, 3], self.s_recv.at[a, 3], self.sibling)
            use(*self.where(da, 2, c))
        for a in range(4):
            from_sibling(a, 3)

    def finish(self):
        for copy in self.started:
            copy.wait_send()


def greet(peers):
    barrier = pltpu.get_barrier_semaphore()
    for peer in peers:
        pl.semaphore_signal(barrier, inc=1, device_id=peer, device_id_type=MESH)
    pl.semaphore_wait(barrier, len(peers))


GROUP = 32


def merge_out_kernel(
    start_a, start_b, begin_b, x_ref, w_own, w_other, text, o_ref, text_rows, hidden, weight, product, t_send, t_recv, w_sem, *sems
):
    torus = Torus(x_ref, hidden, sems)
    z, y, c, x = coords()
    greet(torus.peers() + [device(z, y, c, lax.rem(x + d, 4)) for d in (1, 2, 3)])
    torus.start()
    loads = [
        pltpu.make_async_copy(w_own, weight.at[0], w_sem.at[0]),
        pltpu.make_async_copy(w_other, weight.at[1], w_sem.at[1]),
        pltpu.make_async_copy(text.at[pl.ds(pl.multiple_of(x * 96, 96), 96)], text_rows.at[x], t_send.at[0]),
    ]
    for load in loads:
        load.start()

    def text_copy(d):
        to = lax.rem(x + d, 4)
        return pltpu.make_async_remote_copy(
            src_ref=text.at[pl.ds(pl.multiple_of(to * 96, 96), 96)],
            dst_ref=text_rows.at[x],
            send_sem=t_send.at[d],
            recv_sem=t_recv.at[d],
            device_id=device(z, y, c, to),
            device_id_type=MESH,
        )

    for d in (1, 2, 3):
        text_copy(d).start()
    product[...] = jnp.zeros(product.shape, F32)
    loads[0].wait()
    loads[1].wait()
    own_section = lax.div(y, 2)

    def use(s, q):
        total = jnp.dot(hidden[s, q], weight[lax.rem(s + own_section, 2)], preferred_element_type=F32)
        rows = pl.ds(pl.multiple_of(q * 256, 256), 256)
        for half in range(2):
            product[half, rows, :] += total[:, half * 128 : (half + 1) * 128]

    torus.run(use)
    row = lax.broadcasted_iota(jnp.int32, (GROUP, 128), 0)

    def body(q, carry):
        for m in range(4):
            for k in range(3):
                g = q * 12 + m * 3 + k
                for half in range(2):
                    first = product[half, pl.ds(start_a[g], GROUP), :]
                    second = product[half, pl.ds(start_b[g], GROUP), :]
                    chosen = jnp.where(row >= begin_b[g], second, first).astype(BF16)
                    o_ref[m, k, q, :, half * 128 : (half + 1) * 128] = chosen
        return carry

    lax.fori_loop(0, 16, body, 0)
    torus.finish()
    loads[2].wait()
    for d in (1, 2, 3):
        source = lax.rem(x + 4 - d, 4)
        pltpu.make_async_remote_copy(
            src_ref=text_rows.at[source],
            dst_ref=text_rows.at[source],
            send_sem=t_send.at[d],
            recv_sem=t_recv.at[d],
            device_id=device(z, y, c, source),
            device_id_type=MESH,
        ).wait_recv()
        text_copy(d).wait_send()


def merge_out(hidden, w_own, w_other, text, start_a, start_b, begin_b):
    dma = pltpu.SemaphoreType.DMA
    smem = pl.BlockSpec(memory_space=pltpu.SMEM)
    return pl.pallas_call(
        merge_out_kernel,
        in_specs=[smem, smem, smem, VMEM, ANY, ANY, ANY],
        out_specs=[VMEM, ANY],
        out_shape=[
            jax.ShapeDtypeStruct((4, 3, 16, GROUP, 256), BF16),
            jax.ShapeDtypeStruct((4, 96, 2048), BF16),
        ],
        scratch_shapes=[
            pltpu.VMEM((2, 16, 256, 640), BF16),
            pltpu.VMEM((2, 640, 256), BF16),
            pltpu.VMEM((2, 4096 + GROUP, 128), F32),
            dma((4,)),
            dma((4,)),
            dma((2,)),
        ]
        + torus_sems(),
        compiler_params=pltpu.CompilerParams(
            collective_id=0, has_side_effects=True, vmem_limit_bytes=60 * MIB
        ),
        name="merge_out",
    )(start_a, start_b, begin_b, hidden, w_own, w_other, text)


def spread_kernel(
    part, out_bias, visual_mask, gain, bias, cos_ref, sin_ref, text_ref, wq_ref, wk_ref, wv_ref,
    q_out, kv_out, e_out,
    relay, relayed, got, summed, rows, text, out, normed, wq, wkv, total,
    r_send, r_recv, v_send, v_recv, own_sem, g_send, g_recv, load_sem,
):
    z, y, c, x = coords()
    s, q = place(z, y, c)
    linear = s * 16 + q
    right, left, across = lax.rem(x + 1, 4), lax.rem(x + 3, 4), lax.rem(x + 2, 4)
    to_right, to_left = device(z, y, c, right), device(z, y, c, left)
    pltpu.make_async_copy(text_ref, text, load_sem.at[0]).start()
    pltpu.make_async_copy(wq_ref, wq, load_sem.at[1]).start()

    @pl.when(s == 0)
    def _():
        pltpu.make_async_copy(wk_ref, wkv, load_sem.at[2]).start()

    @pl.when(s == 1)
    def _():
        pltpu.make_async_copy(wv_ref, wkv, load_sem.at[2]).start()

    def peer(j):
        other = lax.rem(linear + j, 32)
        return lax.div(other, 16), lax.rem(other, 16)

    barrier = pltpu.get_barrier_semaphore()
    for to in (to_right, to_left):
        pl.semaphore_signal(barrier, inc=1, device_id=to, device_id_type=MESH)

    def hello(j, carry):
        ps, pq = peer(j)
        pl.semaphore_signal(
            barrier, inc=1, device_id={"section": ps, "seq": pq, "mp": x}, device_id_type=MESH
        )
        return carry

    lax.fori_loop(1, 32, hello, 0)
    pl.semaphore_wait(barrier, 33)

    TOP, BOTTOM = pl.ds(0, 8), pl.ds(8, 8)

    def sum_copy(k, i):
        source, target, to = [
            (part.at[across, k, TOP], relay.at[k, 0], to_right),
            (part.at[across, k, BOTTOM], relay.at[k, 1], to_left),
            (part.at[right, k, BOTTOM], got.at[k, 0, BOTTOM], to_right),
            (part.at[left, k, TOP], got.at[k, 1, TOP], to_left),
            (relayed.at[k, 0], got.at[k, 0, TOP], to_right),
            (relayed.at[k, 1], got.at[k, 1, BOTTOM], to_left),
        ][i]
        return pltpu.make_async_remote_copy(
            src_ref=source,
            dst_ref=target,
            send_sem=r_send.at[k, i],
            recv_sem=r_recv.at[k, i],
            device_id=to,
            device_id_type=MESH,
        )

    def start_sums(k):
        for i in range(4):
            sum_copy(k, i).start()

    def relay_sums(k):
        for i, to, shift in ((0, right, 0), (1, left, 8)):
            sum_copy(k, i).wait_recv()

            def body(j, carry, i=i, to=to, shift=shift):
                both = relay[k, i, j].astype(F32) + part[to, k, j + shift].astype(F32)
                relayed[k, i, j] = both.astype(BF16)
                return carry

            lax.fori_loop(0, 8, body, 0)
            sum_copy(k, 4 + i).start()

    def add_up(k):
        for i in range(2, 6):
            sum_copy(k, i).wait_recv()

        def body(i, carry):
            value = part[x, k, i].astype(F32) + out_bias[...]
            value = value + got[k, 0, i].astype(F32) + got[k, 1, i].astype(F32)
            summed[k, i] = value.astype(BF16)
            return carry

        lax.fori_loop(0, 16, body, 0)

    def start_owner(k):
        def body(j, carry):
            ps, pq = peer(j)
            pltpu.make_async_remote_copy(
                src_ref=summed.at[k, pq],
                dst_ref=rows.at[k, q * 2 + s],
                send_sem=v_send.at[k],
                recv_sem=v_recv.at[k],
                device_id={"section": ps, "seq": pq, "mp": x},
                device_id_type=MESH,
            ).start()
            return carry

        lax.fori_loop(1, 32, body, 0)
        pltpu.make_async_copy(summed.at[k, q], rows.at[k, q * 2 + s], own_sem.at[k]).start()

    def place_rows(k):
        pltpu.make_async_copy(summed.at[k, q], rows.at[k, q * 2 + s], own_sem.at[k]).wait()
        pltpu.make_async_copy(rows.at[k, pl.ds(0, 31)], rows.at[k, pl.ds(0, 31)], v_recv.at[k]).wait()
        visual = visual_mask[k * 32 : (k + 1) * 32, :] > 0.5
        for b in range(32):
            own_text = text[b // 8, k * 32 : (k + 1) * 32, (b % 8) * 256 : (b % 8 + 1) * 256]
            out[k, x, b] = jnp.where(visual, rows[k, b].astype(F32), own_text.astype(F32)).astype(BF16)

    def row_copy(k, piece, origin, to, slot):
        block = out.at[k, origin] if piece is None else out.at[k, origin, pl.ds(piece * 16, 16)]
        return pltpu.make_async_remote_copy(
            src_ref=block,
            dst_ref=block,
            send_sem=g_send.at[k, slot],
            recv_sem=g_recv.at[k, slot],
            device_id=to,
            device_id_type=MESH,
        )

    def start_rows(k):
        row_copy(k, None, x, to_right, 0).start()
        row_copy(k, None, x, to_left, 1).start()

    def relay_rows(k):
        row_copy(k, None, left, to_right, 0).wait_recv()
        row_copy(k, 0, left, to_right, 2).start()
        row_copy(k, None, right, to_left, 1).wait_recv()
        row_copy(k, 1, right, to_left, 3).start()

    def project(k):
        row_copy(k, 0, across, to_right, 2).wait_recv()
        row_copy(k, 1, across, to_left, 3).wait_recv()

        def square(b, carry):
            values = out[k, :, b].reshape(128, 256).astype(F32)
            return carry + values * values

        squares = lax.fori_loop(0, 32, square, jnp.zeros((128, 256), F32), unroll=2)
        mean = jnp.sum(squares, axis=-1, keepdims=True) * (1.0 / 8192.0)
        scale = jnp.broadcast_to(lax.rsqrt(mean + 1e-06), (128, 256))

        total[...] = jnp.broadcast_to(bias[...], total.shape)

        def depth(i, carry):
            for j in range(4):
                b = i * 4 + j
                values = out[k, :, b].reshape(128, 256).astype(F32)
                normed[:, j * 256 : (j + 1) * 256] = (values * scale * gain[b]).astype(BF16)
            span = pl.ds(pl.multiple_of(i * 1024, 1024), 1024)
            total[:, :512] += jnp.dot(normed[...], wq[span, :], preferred_element_type=F32)
            total[:, 512:] += jnp.dot(normed[...], wkv[span, :], preferred_element_type=F32)
            return carry

        lax.fori_loop(0, 8, depth, 0)
        for m in range(4):
            here = slice(m * 32, (m + 1) * 32)
            there = slice(m * 96 + k * 32, m * 96 + (k + 1) * 32)
            cosine, sine = cos_ref[there, :], sin_ref[there, :]

            def rotate(values):
                return (values * cosine + pltpu.roll(values, 64, 1) * sine).astype(BF16)

            for h in range(4):
                cols = slice(h * 128, (h + 1) * 128)
                q_out[there, cols] = rotate(total[here, cols])

            @pl.when(s == 0)
            def _():
                kv_out[there, :] = rotate(total[here, 512:])

            @pl.when(s == 1)
            def _():
                kv_out[there, :] = total[here, 512:].astype(BF16)

            for j in range(8):
                e_out[there, j * 256 : (j + 1) * 256] = out[k, m, x * 8 + j]

    start_sums(0)
    relay_sums(0)
    start_sums(1)
    add_up(0)
    start_owner(0)
    relay_sums(1)
    start_sums(2)
    add_up(1)
    start_owner(1)
    pltpu.make_async_copy(text_ref, text, load_sem.at[0]).wait()
    place_rows(0)
    start_rows(0)
    relay_sums(2)
    add_up(2)
    start_owner(2)
    place_rows(1)
    start_rows(1)
    relay_rows(0)
    place_rows(2)
    start_rows(2)
    relay_rows(1)
    pltpu.make_async_copy(wq_ref, wq, load_sem.at[1]).wait()
    pltpu.make_async_copy(wk_ref, wkv, load_sem.at[2]).wait()
    project(0)
    relay_rows(2)
    project(1)
    project(2)
    for k in range(3):
        for i in range(6):
            sum_copy(k, i).wait_send()
        pltpu.make_async_copy(rows.at[k, pl.ds(0, 31)], rows.at[k, pl.ds(0, 31)], v_send.at[k]).wait()
        row_copy(k, None, x, to_right, 0).wait_send()
        row_copy(k, None, x, to_left, 1).wait_send()
        row_copy(k, 0, left, to_right, 2).wait_send()
        row_copy(k, 1, right, to_left, 3).wait_send()


def spread(part, out_bias, visual_mask, gain, bias, cos, sin, text, wq, wk, wv):
    dma = pltpu.SemaphoreType.DMA
    return pl.pallas_call(
        spread_kernel,
        out_shape=[
            jax.ShapeDtypeStruct((384, 512), BF16),
            jax.ShapeDtypeStruct((384, 128), BF16),
            jax.ShapeDtypeStruct((384, 2048), BF16),
        ],
        in_specs=[VMEM] * 7 + [ANY] * 4,
        out_specs=[VMEM] * 3,
        scratch_shapes=[
            pltpu.VMEM((3, 2, 8, GROUP, 256), BF16),
            pltpu.VMEM((3, 2, 8, GROUP, 256), BF16),
            pltpu.VMEM((3, 2, 16, GROUP, 256), BF16),
            pltpu.VMEM((3, 16, GROUP, 256), BF16),
            pltpu.VMEM((3, 32, GROUP, 256), BF16),
            pltpu.VMEM((4, 96, 2048), BF16),
            pltpu.VMEM((3, 4, 32, GROUP, 256), BF16),
            pltpu.VMEM((128, 1024), BF16),
            pltpu.VMEM((8192, 512), BF16),
            pltpu.VMEM((8192, 128), BF16),
            pltpu.VMEM((128, 640), F32),
            dma((3, 6)),
            dma((3, 6)),
            dma((3,)),
            dma((3,)),
            dma((3,)),
            dma((3, 4)),
            dma((3, 4)),
            dma((3,)),
        ],
        compiler_params=pltpu.CompilerParams(
            collective_id=2, has_side_effects=True, vmem_limit_bytes=60 * MIB
        ),
        name="spread",
    )(part, out_bias, visual_mask, gain, bias, cos, sin, text, wq, wk, wv)


def attention_kernel(q_ref, shard, o_ref, kv_ref, scores, peak, norm, total, *sems):
    torus = Torus(shard, kv_ref, sems)
    greet(torus.peers())
    torus.start()
    torus.run(lambda s, q: None)
    own = lax.axis_index("seq")
    rows = q_ref.shape[0]
    factor = HEAD**-0.5 * math.log2(math.e)

    def stage(h):
        first, second = h < 4, h >= 1
        a, b = h % 2, (h + 1) % 2
        if first:
            query = q_ref[:, h * HEAD : (h + 1) * HEAD]
            peak[a] = jnp.full((rows, 128), -jnp.inf, F32)
        if second:
            top = jnp.broadcast_to(jnp.max(peak[b], axis=1, keepdims=True) * factor, (rows, 128))
            norm[...] = jnp.zeros((rows, 128), F32)
            total[...] = jnp.zeros((rows, HEAD), F32)

        def block(j, masked):
            pair = pl.ds(2 * j, 2)
            if first:
                keys = kv_ref[0, pair].reshape(2 * rows, HEAD)
                found = lax.dot_general(
                    query, keys, (((1,), (1,)), ((), ())), preferred_element_type=F32
                )
                if masked:
                    row = lax.broadcasted_iota(jnp.int32, found.shape, 0)
                    col = lax.broadcasted_iota(jnp.int32, found.shape, 1)
                    found = jnp.where(col - row <= (own - 2 * j) * rows, found, -jnp.inf)
                scores[a, j] = found
                tiles = [found[:, i * 128 : (i + 1) * 128] for i in range(6)]
                high = jnp.maximum(jnp.maximum(tiles[0], tiles[1]), jnp.maximum(tiles[2], tiles[3]))
                peak[a] = jnp.maximum(peak[a], jnp.maximum(high, jnp.maximum(tiles[4], tiles[5])))
            if second:
                tiles = [
                    jnp.exp2(scores[b, j, :, i * 128 : (i + 1) * 128] * factor - top) for i in range(6)
                ]
                norm[...] += ((tiles[0] + tiles[1]) + (tiles[2] + tiles[3])) + (tiles[4] + tiles[5])
                weights = jnp.concatenate([tile.astype(BF16) for tile in tiles], axis=1)
                values = kv_ref[1, pair].reshape(2 * rows, HEAD)
                total[...] += jnp.dot(weights, values, preferred_element_type=F32)

        def body(j, carry):
            block(j, False)
            return carry

        last = lax.div(own, 2)
        lax.fori_loop(0, last, body, 0)
        block(last, True)
        if second:
            cols = slice((h - 1) * HEAD, h * HEAD)
            o_ref[:, cols] = (total[...] / jnp.sum(norm[...], axis=1, keepdims=True)).astype(BF16)

    for h in range(5):
        stage(h)
    torus.finish()


def attention(queries, shard):
    rows = queries.shape[0]
    return pl.pallas_call(
        attention_kernel,
        out_shape=jax.ShapeDtypeStruct(queries.shape, BF16),
        in_specs=[VMEM, VMEM],
        out_specs=VMEM,
        scratch_shapes=[
            pltpu.VMEM((2, 16, rows, HEAD), BF16),
            pltpu.VMEM((2, 8, rows, 2 * rows), F32),
            pltpu.VMEM((2, rows, HEAD), F32),
            pltpu.VMEM((rows, HEAD), F32),
            pltpu.VMEM((rows, HEAD), F32),
        ]
        + torus_sems(),
        compiler_params=pltpu.CompilerParams(
            collective_id=1, has_side_effects=True, vmem_limit_bytes=60 * MIB
        ),
        name="attention",
    )(queries, shard)


def local(
    patches,
    norm_gain,
    norm_shift,
    merge_in_weight,
    merge_in_bias,
    merge_out_weight,
    merge_out_bias,
    text_embeds,
    rms_gain,
    query_weight,
    query_bias,
    key_weight,
    key_bias,
    value_weight,
    value_bias,
    patch_counts,
    image_offsets,
):
    section = lax.axis_index("section")
    seq = lax.axis_index("seq")
    col = lax.axis_index("mp")
    own_rows = text_embeds.shape[0]
    tokens = patch_counts // 4
    first = jnp.arange(6144 // GROUP, dtype=jnp.int32) * GROUP
    image_a = jnp.sum((image_offsets[None, :] <= first[:, None]).astype(jnp.int32), axis=1) - 1
    image_b = jnp.minimum(image_a + 1, 15)
    pick_a = image_a[:, None] == jnp.arange(16, dtype=jnp.int32)[None, :]
    pick_b = image_b[:, None] == jnp.arange(16, dtype=jnp.int32)[None, :]
    offset_a = jnp.sum(jnp.where(pick_a, image_offsets[None, :], 0), axis=1)
    offset_b = jnp.sum(jnp.where(pick_b, image_offsets[None, :], 0), axis=1)
    begin_b = jnp.where(image_a == 15, GROUP, jnp.minimum(offset_b - first, GROUP))
    start_a = jnp.minimum(image_a * 256 + first - offset_a, 4096)
    start_b = image_b * 256 - begin_b
    own_positions = seq * own_rows + jnp.arange(own_rows, dtype=jnp.int32)
    block_positions = seq * own_rows + col * 96 + jnp.arange(96, dtype=jnp.int32)
    relative = block_positions[:, None] - image_offsets[None, :]
    is_visual = jnp.any((relative >= 0) & (relative < tokens[None, :]), axis=1)
    visual_mask = jnp.broadcast_to(is_visual[:, None].astype(F32), (96, 256))
    half_dim = HEAD // 2
    inv_freq = jnp.exp(jnp.arange(half_dim, dtype=F32) * (-2.0 * math.log(1000000.0) / HEAD))
    angles = own_positions.astype(F32)[:, None] * inv_freq[None, :]
    cosine, sine = jnp.cos(angles), jnp.sin(angles)
    cos_table = jnp.concatenate([cosine, cosine], axis=1)
    sin_table = jnp.concatenate([-sine, sine], axis=1)

    halves = merge_out_weight.reshape(merge_out_weight.shape[0], 2, 256)
    w_own = lax.dynamic_index_in_dim(halves, section, 1, keepdims=False)
    w_other = lax.ppermute(
        lax.dynamic_index_in_dim(halves, 1 - section, 1, keepdims=False), "section", [(0, 1), (1, 0)]
    )
    hidden = merge_in(patches, norm_gain, norm_shift, merge_in_weight, merge_in_bias)
    part, text_rows = merge_out(hidden, w_own, w_other, text_embeds, start_a, start_b, begin_b)
    out_bias = lax.dynamic_slice_in_dim(merge_out_bias, section * 256, 256, 0).astype(F32)[None, :]
    key_value_bias = jnp.where(section == 0, key_bias, value_bias)
    bias = jnp.concatenate([query_bias, key_value_bias]).astype(F32)[None, :]
    gain = rms_gain.astype(F32).reshape(32, 1, 256)
    queries, shard, embeds = spread(
        part,
        out_bias,
        visual_mask,
        gain,
        bias,
        cos_table,
        sin_table,
        text_rows,
        query_weight,
        key_weight,
        value_weight,
    )
    return (embeds, attention(queries, shard))


def solution(mesh):
    placed = (
        P("seq", None),
        P(),
        P(),
        P(None, ("section", "mp")),
        P(("section", "mp")),
        P(("section", "mp"), "seq"),
        P("seq"),
        P("seq", "mp"),
        P(),
        P(None, ("section", "mp")),
        P(("section", "mp")),
        P(None, "mp"),
        P("mp"),
        P(None, "mp"),
        P("mp"),
        P(),
        P(),
    )
    return jax.shard_map(
        local,
        mesh=mesh,
        in_specs=placed,
        out_specs=(P("seq", "mp"), P("seq", ("section", "mp"))),
        check_vma=False,
    )
```

```python
import math

import jax
import jax.numpy as jnp
from jax import lax
from jax.experimental import pallas as pl
from jax.experimental.pallas import tpu as pltpu
from jax.sharding import PartitionSpec as P

HEAD = 128
MESH = pl.DeviceIdType.MESH
MIB = 1024 * 1024
ANY = pl.BlockSpec(memory_space=pl.ANY)
VMEM = pl.BlockSpec(memory_space=pltpu.VMEM)
BF16 = jnp.bfloat16
F32 = jnp.float32


def coords():
    s = lax.axis_index("section")
    q = lax.axis_index("seq")
    z = lax.div(q, 4)
    y = s * 2 + lax.rem(lax.div(q, 2), 2)
    return z, y, lax.rem(q, 2), lax.axis_index("mp")


def place(z, y, c):
    return lax.div(y, 2), z * 4 + lax.rem(y, 2) * 2 + c


def device(z, y, c, x):
    s, q = place(z, y, c)
    return {"section": s, "seq": q, "mp": x}


def torus_sems():
    dma = pltpu.SemaphoreType.DMA
    return [dma((4,)), dma((4,)), dma((4, 4)), dma((4, 4)), dma((4, 4)), dma((4, 4)), dma]


class Torus:
    def __init__(self, x_ref, out_ref, sems, base, count):
        self.x_ref, self.out_ref = x_ref.at[pl.ds(base, count)], out_ref
        self.base, self.count = base, count
        self.a_send, self.a_recv, self.b_send, self.b_recv, self.s_send, self.s_recv, self.own_sem = sems
        self.z, self.y, self.c, self.x = coords()
        self.half = count // 2
        self.started = []
        self.sibling = device(self.z, self.y, 1 - self.c, self.x)

    def where(self, da, db, core):
        zz = lax.rem(self.z + da * (1 - core) + db * core + 8, 4)
        yy = lax.rem(self.y + da * core + db * (1 - core) + 8, 4)
        return place(zz, yy, core)

    def target(self, da, db):
        s, q = self.where(da, db, self.c)
        return {"section": s, "seq": q, "mp": self.x}

    def peers(self):
        return [self.target(1, 0), self.target(-1, 0), self.target(0, 1), self.target(0, -1), self.sibling]

    def view(self, da, db, core, part):
        s, q = self.where(da, db, core)
        if part is None:
            return self.out_ref.at[s, q, pl.ds(self.base, self.count)]
        return self.out_ref.at[s, q, pl.ds(self.base + part * self.half, self.half)]

    def send(self, da, db, part, send_sem, recv_sem, to):
        block = self.view(da, db, self.c, part)
        copy = pltpu.make_async_remote_copy(
            src_ref=self.x_ref if da == 0 and db == 0 else block,
            dst_ref=block,
            send_sem=send_sem,
            recv_sem=recv_sem,
            device_id=to,
            device_id_type=MESH,
        )
        copy.start()
        self.started.append(copy)

    def arrived(self, da, db, core, part, send_sem, recv_sem):
        block = self.view(da, db, core, part)
        pltpu.make_async_remote_copy(
            src_ref=block,
            dst_ref=block,
            send_sem=send_sem,
            recv_sem=recv_sem,
            device_id=self.sibling,
            device_id_type=MESH,
        ).wait_recv()

    def along_b(self, a, da):
        self.send(da, 0, None, self.b_send.at[a, 0], self.b_recv.at[a, 0], self.target(0, 1))
        self.send(da, 0, None, self.b_send.at[a, 1], self.b_recv.at[a, 1], self.target(0, -1))
        self.send(da, 0, None, self.s_send.at[a, 0], self.s_recv.at[a, 0], self.sibling)

    def start(self):
        self.send(0, 0, None, self.a_send.at[0], self.a_recv.at[0], self.target(1, 0))
        self.send(0, 0, None, self.a_send.at[1], self.a_recv.at[1], self.target(-1, 0))
        self.along_b(0, 0)
        self.own_copy = pltpu.make_async_copy(self.x_ref, self.view(0, 0, self.c, None), self.own_sem)
        self.own_copy.start()

    def run(self, use):
        offsets = [0, -1, 1, 2]
        c = self.c

        def from_sibling(a, b):
            da, db = offsets[a], offsets[b]
            self.arrived(da, db, 1 - c, None, self.s_send.at[a, b], self.s_recv.at[a, b])
            use(*self.where(da, db, 1 - c))

        def relay_b(a):
            da = offsets[a]
            self.arrived(da, -1, c, None, self.b_send.at[a, 0], self.b_recv.at[a, 0])
            self.send(da, -1, 0, self.b_send.at[a, 2], self.b_recv.at[a, 2], self.target(0, 1))
            self.send(da, -1, None, self.s_send.at[a, 1], self.s_recv.at[a, 1], self.sibling)
            self.arrived(da, 1, c, None, self.b_send.at[a, 1], self.b_recv.at[a, 1])
            self.send(da, 1, 1, self.b_send.at[a, 3], self.b_recv.at[a, 3], self.target(0, -1))
            self.send(da, 1, None, self.s_send.at[a, 2], self.s_recv.at[a, 2], self.sibling)
            use(*self.where(da, -1, c))
            use(*self.where(da, 1, c))

        self.own_copy.wait()
        use(*self.where(0, 0, c))
        self.arrived(-1, 0, c, None, self.a_send.at[0], self.a_recv.at[0])
        self.send(-1, 0, 0, self.a_send.at[2], self.a_recv.at[2], self.target(1, 0))
        self.along_b(1, -1)
        self.arrived(1, 0, c, None, self.a_send.at[1], self.a_recv.at[1])
        self.send(1, 0, 1, self.a_send.at[3], self.a_recv.at[3], self.target(-1, 0))
        self.along_b(2, 1)
        use(*self.where(-1, 0, c))
        use(*self.where(1, 0, c))
        from_sibling(0, 0)
        yield
        relay_b(0)
        yield
        self.arrived(2, 0, c, 0, self.a_send.at[2], self.a_recv.at[2])
        self.arrived(2, 0, c, 1, self.a_send.at[3], self.a_recv.at[3])
        self.along_b(3, 2)
        use(*self.where(2, 0, c))
        from_sibling(1, 0)
        from_sibling(2, 0)
        for a in (1, 2, 3):
            relay_b(a)
            from_sibling(a - 1, 1)
            from_sibling(a - 1, 2)
            yield
        from_sibling(3, 0)
        from_sibling(3, 1)
        from_sibling(3, 2)
        for a in range(4):
            da = offsets[a]
            self.arrived(da, 2, c, 0, self.b_send.at[a, 2], self.b_recv.at[a, 2])
            self.arrived(da, 2, c, 1, self.b_send.at[a, 3], self.b_recv.at[a, 3])
            self.send(da, 2, None, self.s_send.at[a, 3], self.s_recv.at[a, 3], self.sibling)
            use(*self.where(da, 2, c))
        for a in range(4):
            from_sibling(a, 3)

    def finish(self):
        for copy in self.started:
            copy.wait_send()


def greet(peers):
    barrier = pltpu.get_barrier_semaphore()
    for peer in peers:
        pl.semaphore_signal(barrier, inc=1, device_id=peer, device_id_type=MESH)
    pl.semaphore_wait(barrier, len(peers))


class CrossSum:
    def __init__(self, staged, relay, relayed, got, sums, bias, send_sem, recv_sem):
        self.staged, self.relay, self.relayed, self.got, self.sums = staged, relay, relayed, got, sums
        self.bias, self.send_sem, self.recv_sem = bias, send_sem, recv_sem
        z, y, c, x = coords()
        self.x = x
        self.right, self.left, self.across = lax.rem(x + 1, 4), lax.rem(x + 3, 4), lax.rem(x + 2, 4)
        self.to_right, self.to_left = device(z, y, c, self.right), device(z, y, c, self.left)

    def copy(self, g, i):
        top, bottom = pl.ds(0, 128), pl.ds(128, 128)
        staged, got, sums = self.staged.at[g], self.got.at[g], self.sums.at[g]
        source, target, to = [
            (staged.at[self.across, top], self.relay.at[g, 0], self.to_right),
            (staged.at[self.across, bottom], self.relay.at[g, 1], self.to_left),
            (staged.at[self.right, bottom], got.at[0, bottom], self.to_right),
            (staged.at[self.left, top], got.at[1, top], self.to_left),
            (self.relayed.at[g, 0], got.at[0, top], self.to_right),
            (self.relayed.at[g, 1], got.at[1, bottom], self.to_left),
            (sums.at[self.x], sums.at[self.x], self.to_right),
            (sums.at[self.x], sums.at[self.x], self.to_left),
            (sums.at[self.left, top], sums.at[self.left, top], self.to_right),
            (sums.at[self.right, bottom], sums.at[self.right, bottom], self.to_left),
        ][i]
        return pltpu.make_async_remote_copy(
            src_ref=source,
            dst_ref=target,
            send_sem=self.send_sem.at[g, i],
            recv_sem=self.recv_sem.at[g, i],
            device_id=to,
            device_id_type=MESH,
        )

    def landed(self, g, origin, part, i):
        block = self.sums.at[g, origin] if part is None else self.sums.at[g, origin, pl.ds(part * 128, 128)]
        pltpu.make_async_remote_copy(
            src_ref=block,
            dst_ref=block,
            send_sem=self.send_sem.at[g, i],
            recv_sem=self.recv_sem.at[g, i],
            device_id=self.to_right,
            device_id_type=MESH,
        ).wait_recv()

    def start(self, g):
        for i in range(4):
            self.copy(g, i).start()

    def pass_on(self, g):
        for i, to in ((0, self.right), (1, self.left)):
            self.copy(g, i).wait_recv()

            def body(j, carry, i=i, to=to):
                here = pl.ds(pl.multiple_of(j * 32, 32), 32)
                there = pl.ds(pl.multiple_of(j * 32 + i * 128, 32), 32)
                both = self.relay[g, i, here, :].astype(F32) + self.staged[g, to, there, :].astype(F32)
                self.relayed[g, i, here, :] = both.astype(BF16)
                return carry

            lax.fori_loop(0, 4, body, 0)
            self.copy(g, 4 + i).start()

    def add_up(self, g):
        for i in range(2, 6):
            self.copy(g, i).wait_recv()

        def body(j, carry):
            here = pl.ds(pl.multiple_of(j * 32, 32), 32)
            value = self.staged[g, self.x, here, :].astype(F32) + self.bias
            value = value + self.got[g, 0, here, :].astype(F32) + self.got[g, 1, here, :].astype(F32)
            self.sums[g, self.x, here, :] = value.astype(BF16)
            return carry

        lax.fori_loop(0, 8, body, 0)
        self.copy(g, 6).start()
        self.copy(g, 7).start()

    def spread(self, g):
        self.landed(g, self.left, None, 6)
        self.copy(g, 8).start()
        self.landed(g, self.right, None, 7)
        self.copy(g, 9).start()

    def done(self, g):
        self.landed(g, self.across, 0, 8)
        self.landed(g, self.across, 1, 9)

    def finish(self, g):
        for i in range(10):
            self.copy(g, i).wait_send()


GROUP = 32


def merger_kernel(
    offsets, vecs, patches_ref, w_in_ref, w_out_ref, text,
    part, text_rows, text_last,
    x_buf, w_in, normed, joined, shard, hidden, weight, product, staged, relay, relayed, got, sums,
    t_send, t_recv, w_sem, c_send, c_recv, *sems
):
    halves = [Torus(shard, hidden, sems[h * 7 : h * 7 + 7], h * 128, 128) for h in range(2)]
    z, y, c, x = coords()
    section = lax.div(y, 2)
    cross = CrossSum(
        staged, relay, relayed, got, sums,
        vecs[:, pl.ds(pl.multiple_of(3200 + section * 256, 128), 256)], c_send, c_recv,
    )
    load_x = [
        pltpu.make_async_copy(patches_ref.at[pl.ds(h * 512, 512)], x_buf.at[pl.ds(h * 512, 512)], w_sem.at[5 + h])
        for h in range(2)
    ]
    load_w = [
        pltpu.make_async_copy(w_in_ref.at[pl.ds(i * 1280, 1280)], w_in.at[pl.ds(i * 1280, 1280)], w_sem.at[7 + i])
        for i in range(4)
    ]
    for load in load_x + load_w:
        load.start()
    other = device(z, lax.rem(y + 2, 4), c, x)
    greet(halves[0].peers() + [device(z, y, c, lax.rem(x + d, 4)) for d in (1, 2, 3)] + [other])

    def half_of(s):
        return w_out_ref.at[:, pl.ds(pl.multiple_of(s * 256, 256), 256)]

    swap = pltpu.make_async_remote_copy(
        src_ref=half_of(1 - section),
        dst_ref=weight.at[1],
        send_sem=w_sem.at[2],
        recv_sem=w_sem.at[3],
        device_id=other,
        device_id_type=MESH,
    )
    swap.start()
    keep = pltpu.make_async_copy(half_of(section), weight.at[0], w_sem.at[4])
    keep.start()

    def text_copy(d, last):
        to = lax.rem(x + d, 4)
        if last:
            source, target = text.at[pl.ds(256, 128)], text_last.at[x]
        else:
            source, target = text.at[pl.ds(pl.multiple_of(to * 64, 64), 64)], text_rows.at[x]
        return pltpu.make_async_remote_copy(
            src_ref=source,
            dst_ref=target,
            send_sem=t_send.at[last, d],
            recv_sem=t_recv.at[last, d],
            device_id=device(z, y, c, to),
            device_id_type=MESH,
        )

    for last in (0, 1):
        for d in (1, 2, 3):
            text_copy(d, last).start()

    width = patches_ref.shape[1]
    tiles = width // 128
    gain, shift = vecs[:, :1280], vecs[:, 1280:2560]
    def norm(h, first, last):
        def body(i, carry):
            from_row = pl.ds(pl.multiple_of(h * 512 + i * 64, 64), 64)
            to_row = pl.ds(pl.multiple_of(i * 64, 64), 64)
            values = x_buf[from_row, :].astype(F32)
            center = values - jnp.mean(values, axis=-1, keepdims=True)
            spread = jnp.mean(center * center, axis=-1, keepdims=True)
            result = center * lax.rsqrt(spread + 1e-06) * gain + shift
            for u in range(tiles):
                normed[u, to_row, :] = result[:, u * 128 : (u + 1) * 128]
            return carry

        lax.fori_loop(first, last, body, 0)

    def join():
        for t in range(4):
            for u in range(tiles):
                cols = slice((t * tiles + u) * 128, (t * tiles + u + 1) * 128)
                joined[:, cols] = normed[u, pl.ds(t, 128, stride=4), :].astype(BF16)

    def multiply(h, first):
        cols = slice(first, min(first + 256, 640))
        total = jnp.dot(joined[...], w_in[:, cols], preferred_element_type=F32)
        total = total + vecs[:, 2560 + cols.start : 2560 + cols.stop]
        shard[h * 128 : (h + 1) * 128, cols] = (0.5 * total * (1.0 + lax.erf(total * (2.0**-0.5)))).astype(BF16)

    def use(h):
        def multiply_out(s, q):
            block = hidden[s, q, h * 128 : (h + 1) * 128, :]
            total = jnp.dot(block, weight[lax.rem(s + section, 2)], preferred_element_type=F32)
            rows = pl.ds(pl.multiple_of(q * 256 + h * 128, 128), 128)
            for half in range(2):
                product[half, rows, :] += total[:, half * 128 : (half + 1) * 128]

        return multiply_out

    runs = [halves[h].run(use(h)) for h in range(2)]
    load_x[0].wait()
    norm(0, 0, 8)
    join()
    for load in load_w:
        load.wait()
    for first in (0, 256, 512):
        multiply(0, first)
    halves[0].start()
    product[...] = jnp.zeros(product.shape, F32)
    load_x[1].wait()
    norm(1, 0, 8)
    keep.wait()
    swap.wait()
    next(runs[0])
    join()
    multiply(1, 0)
    next(runs[0])
    multiply(1, 256)
    multiply(1, 512)
    next(runs[0])
    next(runs[0])
    halves[1].start()
    for _ in runs[0]:
        pass

    def rows_of(g, n, m):
        return pl.ds((g % 2 * 8 + n) * 256 + g // 2 * 128 + m * 32, 32)

    def stage(g):
        for n in range(8):
            for m in range(4):
                for half in range(2):
                    cols = slice(half * 128, (half + 1) * 128)
                    staged[g, m, n * 32 : (n + 1) * 32, cols] = product[half, rows_of(g, n, m), :].astype(BF16)
        cross.start(g)

    def unstage(g):
        cross.done(g)
        for n in range(8):
            for m in range(4):
                for half in range(2):
                    cols = slice(half * 128, (half + 1) * 128)
                    product[half, rows_of(g, n, m), :] = sums[g, m, n * 32 : (n + 1) * 32, cols].astype(F32)

    stage(0)
    stage(1)
    next(runs[1])
    next(runs[1])
    cross.pass_on(0)
    cross.pass_on(1)
    next(runs[1])
    next(runs[1])
    cross.add_up(0)
    cross.add_up(1)
    next(runs[1])
    cross.spread(0)
    cross.spread(1)
    for _ in runs[1]:
        pass
    stage(2)
    stage(3)
    unstage(0)
    unstage(1)
    cross.pass_on(2)
    cross.pass_on(3)
    cross.add_up(2)
    cross.add_up(3)
    cross.spread(2)
    cross.spread(3)
    unstage(2)
    unstage(3)
    row = lax.broadcasted_iota(jnp.int32, (GROUP, 128), 0)

    def body(q, image_a):
        for i in range(12):
            k, m = (i % 2, i // 2) if i < 8 else (2, i - 8)
            first = q * 384 + i * GROUP
            following = jnp.minimum(image_a + 1, 15)
            image_a = jnp.where(offsets[following] <= first, following, image_a)
            image_b = jnp.minimum(image_a + 1, 15)
            begin = jnp.where(image_a == 15, GROUP, jnp.clip(offsets[image_b] - first, 0, GROUP))
            start_a = jnp.clip(image_a * 256 + first - offsets[image_a], 0, 4096)
            start_b = jnp.clip(image_b * 256 - begin, 0, 4096)
            for half in range(2):
                one = product[half, pl.ds(start_a, GROUP), :]
                two = product[half, pl.ds(start_b, GROUP), :]
                cols = slice(half * 128, (half + 1) * 128)
                part[k, q, m, :, cols] = jnp.where(row >= begin, two, one).astype(BF16)
        return image_a

    lax.fori_loop(0, 16, body, jnp.int32(0))
    for torus in halves:
        torus.finish()
    for g in range(4):
        cross.finish(g)
    for last, target in ((0, text_rows), (1, text_last)):
        for d in (1, 2, 3):
            block = target.at[lax.rem(x + 4 - d, 4)]
            pltpu.make_async_remote_copy(
                src_ref=block,
                dst_ref=block,
                send_sem=t_send.at[last, d],
                recv_sem=t_recv.at[last, d],
                device_id=other,
                device_id_type=MESH,
            ).wait_recv()
            text_copy(d, last).wait_send()


def merger(offsets, vecs, patches, w_in, w_out, text):
    dma = pltpu.SemaphoreType.DMA
    return pl.pallas_call(
        merger_kernel,
        in_specs=[pl.BlockSpec(memory_space=pltpu.SMEM), VMEM, ANY, ANY, ANY, ANY],
        out_specs=[VMEM, ANY, ANY],
        out_shape=[
            jax.ShapeDtypeStruct((3, 16, 4, GROUP, 256), BF16),
            jax.ShapeDtypeStruct((4, 64, 2048), BF16),
            jax.ShapeDtypeStruct((4, 128, 2048), BF16),
        ],
        scratch_shapes=[
            pltpu.VMEM((1024, 1280), BF16),
            pltpu.VMEM((5120, 640), BF16),
            pltpu.VMEM((10, 512, 128), F32),
            pltpu.VMEM((128, 5120), BF16),
            pltpu.VMEM((256, 640), BF16),
            pltpu.VMEM((2, 16, 256, 640), BF16),
            pltpu.VMEM((2, 640, 256), BF16),
            pltpu.VMEM((2, 4096 + GROUP, 128), F32),
            pltpu.VMEM((4, 4, 256, 256), BF16),
            pltpu.VMEM((4, 2, 128, 256), BF16),
            pltpu.VMEM((4, 2, 128, 256), BF16),
            pltpu.VMEM((4, 2, 256, 256), BF16),
            pltpu.VMEM((4, 4, 256, 256), BF16),
            dma((2, 4)),
            dma((2, 4)),
            dma((11,)),
            dma((4, 10)),
            dma((4, 10)),
        ]
        + torus_sems()
        + torus_sems(),
        compiler_params=pltpu.CompilerParams(
            collective_id=0, has_side_effects=True, vmem_limit_bytes=60 * MIB
        ),
        name="merger",
    )(offsets, vecs, patches, w_in, w_out, text)


def spread_kernel(
    offsets, counts, vecs, cos_ref, sin_ref, part, text_ref, text_last_ref, own_text, wq_ref, wk_ref, wv_ref,
    q_out, kv_out, e_hbm,
    e_out, rows, rows_last, text, text_last, out, normed, wq, wkv, total,
    v_send, v_recv, own_sem, g_send, g_recv, load_sem, text_sem,
):
    z, y, c, x = coords()
    s, q = place(z, y, c)
    linear = s * 16 + q
    right, left, across = lax.rem(x + 1, 4), lax.rem(x + 3, 4), lax.rem(x + 2, 4)
    to_right, to_left = device(z, y, c, right), device(z, y, c, left)
    load_text, load_last = [], []
    for d in range(4):
        slot = lax.rem(x + d, 4)
        near, last = text_ref.at[slot], text_last_ref.at[slot]
        if d == 0:
            near = own_text.at[pl.ds(pl.multiple_of(x * 64, 64), 64)]
            last = own_text.at[pl.ds(256, 128)]
        load_text.append(pltpu.make_async_copy(near, text.at[slot], text_sem.at[0, d]))
        load_last.append(pltpu.make_async_copy(last, text_last.at[slot], text_sem.at[1, d]))
    load_q = pltpu.make_async_copy(wq_ref, wq, load_sem.at[1])
    for load in load_text + load_last + [load_q]:
        load.start()

    @pl.when(s == 0)
    def _():
        pltpu.make_async_copy(wk_ref, wkv, load_sem.at[2]).start()

    @pl.when(s == 1)
    def _():
        pltpu.make_async_copy(wv_ref, wkv, load_sem.at[2]).start()

    def peer(j):
        other = lax.rem(linear + j, 32)
        return lax.div(other, 16), lax.rem(other, 16)

    barrier = pltpu.get_barrier_semaphore()
    for to in (to_right, to_left):
        pl.semaphore_signal(barrier, inc=1, device_id=to, device_id_type=MESH)

    def hello(j, carry):
        ps, pq = peer(j)
        pl.semaphore_signal(
            barrier, inc=1, device_id={"section": ps, "seq": pq, "mp": x}, device_id_type=MESH
        )
        return carry

    lax.fori_loop(1, 32, hello, 0)
    pl.semaphore_wait(barrier, 33)

    def own_copy(k):
        if k < 2:
            return pltpu.make_async_copy(part.at[k, q, x], rows.at[k, q * 2 + s], own_sem.at[k])
        return pltpu.make_async_copy(part.at[k, q], rows_last.at[q * 2 + s], own_sem.at[k])

    def start_owner(k):
        def body(j, carry):
            ps, pq = peer(j)
            pltpu.make_async_remote_copy(
                src_ref=part.at[k, pq, x] if k < 2 else part.at[k, pq],
                dst_ref=rows.at[k, q * 2 + s] if k < 2 else rows_last.at[q * 2 + s],
                send_sem=v_send.at[k],
                recv_sem=v_recv.at[k],
                device_id={"section": ps, "seq": pq, "mp": x},
                device_id_type=MESH,
            ).start()
            return carry

        lax.fori_loop(1, 32, body, 0)
        own_copy(k).start()

    def visual_rows(first):
        position = q * 384 + first + lax.broadcasted_iota(jnp.int32, (GROUP, 256), 0)
        found = jnp.zeros((GROUP, 256), jnp.int32)
        for i in range(16):
            begin = offsets[i]
            inside = (position >= begin) & (position < begin + lax.div(counts[i], 4))
            found = jnp.where(inside, 1, found)
        return found > 0

    def others(k):
        return rows.at[k, pl.ds(0, 31)] if k < 2 else rows_last.at[pl.ds(0, 31)]

    def place_rows(k):
        own_copy(k).wait()
        pltpu.make_async_copy(others(k), others(k), v_recv.at[k]).wait()
        if k < 2:
            visual = visual_rows(x * 64 + k * 32)
            for b in range(32):
                own_text = text[b // 8, k * 32 : (k + 1) * 32, (b % 8) * 256 : (b % 8 + 1) * 256]
                out[k, x, b] = jnp.where(visual, rows[k, b].astype(F32), own_text.astype(F32)).astype(BF16)
        else:
            for m in range(4):
                visual = visual_rows(256 + m * 32)
                for b in range(32):
                    own_text = text_last[b // 8, m * 32 : (m + 1) * 32, (b % 8) * 256 : (b % 8 + 1) * 256]
                    picked = jnp.where(visual, rows_last[b, m].astype(F32), own_text.astype(F32))
                    out[k, m, b] = picked.astype(BF16)

    def row_copy(k, piece, origin, to, slot):
        block = out.at[k, origin] if piece is None else out.at[k, origin, pl.ds(piece * 16, 16)]
        return pltpu.make_async_remote_copy(
            src_ref=block,
            dst_ref=block,
            send_sem=g_send.at[k, slot],
            recv_sem=g_recv.at[k, slot],
            device_id=to,
            device_id_type=MESH,
        )

    def start_rows(k):
        row_copy(k, None, x, to_right, 0).start()
        row_copy(k, None, x, to_left, 1).start()

    def relay_rows(k):
        row_copy(k, None, left, to_right, 0).wait_recv()
        row_copy(k, 0, left, to_right, 2).start()
        row_copy(k, None, right, to_left, 1).wait_recv()
        row_copy(k, 1, right, to_left, 3).start()

    def project(k):
        if k < 2:
            row_copy(k, 0, across, to_right, 2).wait_recv()
            row_copy(k, 1, across, to_left, 3).wait_recv()

        def square(b, carry):
            values = out[k, :, b].reshape(128, 256).astype(F32)
            return carry + values * values

        squares = lax.fori_loop(0, 32, square, jnp.zeros((128, 256), F32), unroll=2)
        mean = jnp.sum(squares, axis=-1, keepdims=True) * (1.0 / 8192.0)
        scale = jnp.broadcast_to(lax.rsqrt(mean + 1e-06), (128, 256))

        total[...] = jnp.broadcast_to(vecs[:, 3712:4352], total.shape)

        def depth(i, carry):
            for j in range(4):
                b = i * 4 + j
                values = out[k, :, b].reshape(128, 256).astype(F32)
                gain = vecs[:, pl.ds(pl.multiple_of(4352 + b * 256, 128), 256)]
                normed[:, j * 256 : (j + 1) * 256] = (values * scale * gain).astype(BF16)
            span = pl.ds(pl.multiple_of(i * 1024, 1024), 1024)
            total[:, :512] += jnp.dot(normed[...], wq[span, :], preferred_element_type=F32)
            total[:, 512:] += jnp.dot(normed[...], wkv[span, :], preferred_element_type=F32)
            return carry

        lax.fori_loop(0, 8, depth, 0)
        for m in range(4):
            here = slice(m * 32, (m + 1) * 32)
            there = pl.ds(m * 64 + k * 32 if k < 2 else 256 + m * 32, 32)
            cosine, sine = cos_ref[there, :], sin_ref[there, :]

            def rotate(values):
                return (values * cosine + pltpu.roll(values, 64, 1) * sine).astype(BF16)

            for h in range(4):
                cols = slice(h * 128, (h + 1) * 128)
                q_out[there, cols] = rotate(total[here, cols])

            @pl.when(s == 0)
            def _():
                kv_out[there, :] = rotate(total[here, 512:])

            @pl.when(s == 1)
            def _():
                kv_out[there, :] = total[here, 512:].astype(BF16)

            for j in range(8):
                e_out[there, j * 256 : (j + 1) * 256] = out[k, m, x * 8 + j]

    for k in range(3):
        start_owner(k)
    for load in load_text:
        load.wait()
    place_rows(0)
    start_rows(0)
    place_rows(1)
    start_rows(1)
    relay_rows(0)
    for load in load_last:
        load.wait()
    place_rows(2)
    relay_rows(1)
    load_q.wait()
    pltpu.make_async_copy(wk_ref, wkv, load_sem.at[2]).wait()
    project(2)
    project(0)
    project(1)
    save = pltpu.make_async_copy(e_out, e_hbm, load_sem.at[4])
    save.start()
    for k in range(3):
        pltpu.make_async_copy(others(k), others(k), v_send.at[k]).wait()
    for k in range(2):
        row_copy(k, None, x, to_right, 0).wait_send()
        row_copy(k, None, x, to_left, 1).wait_send()
        row_copy(k, 0, left, to_right, 2).wait_send()
        row_copy(k, 1, right, to_left, 3).wait_send()
    save.wait()


def spread(offsets, counts, vecs, cos, sin, part, text, text_last, own_text, wq, wk, wv):
    dma = pltpu.SemaphoreType.DMA
    smem = pl.BlockSpec(memory_space=pltpu.SMEM)
    return pl.pallas_call(
        spread_kernel,
        out_shape=[
            jax.ShapeDtypeStruct((384, 512), BF16),
            jax.ShapeDtypeStruct((384, 128), BF16),
            jax.ShapeDtypeStruct((384, 2048), BF16),
        ],
        in_specs=[smem, smem, VMEM, VMEM, VMEM, VMEM] + [ANY] * 6,
        out_specs=[VMEM, VMEM, ANY],
        scratch_shapes=[
            pltpu.VMEM((384, 2048), BF16),
            pltpu.VMEM((2, 32, GROUP, 256), BF16),
            pltpu.VMEM((32, 4, GROUP, 256), BF16),
            pltpu.VMEM((4, 64, 2048), BF16),
            pltpu.VMEM((4, 128, 2048), BF16),
            pltpu.VMEM((3, 4, 32, GROUP, 256), BF16),
            pltpu.VMEM((128, 1024), BF16),
            pltpu.VMEM((8192, 512), BF16),
            pltpu.VMEM((8192, 128), BF16),
            pltpu.VMEM((128, 640), F32),
            dma((3,)),
            dma((3,)),
            dma((3,)),
            dma((2, 4)),
            dma((2, 4)),
            dma((5,)),
            dma((2, 4)),
        ],
        compiler_params=pltpu.CompilerParams(
            collective_id=2, has_side_effects=True, vmem_limit_bytes=60 * MIB
        ),
        name="spread",
    )(offsets, counts, vecs, cos, sin, part, text, text_last, own_text, wq, wk, wv)


def attention_kernel(q_ref, shard, o_ref, kv_ref, scores, peak, *sems):
    torus = Torus(shard, kv_ref, sems, 0, shard.shape[0])
    greet(torus.peers())
    torus.start()
    own = lax.axis_index("seq")
    rows = q_ref.shape[0]
    factor = HEAD**-0.5 * math.log2(math.e)
    peak[...] = jnp.full(peak.shape, -jnp.inf, F32)

    def score(j, masked):
        for h in range(4):
            query = q_ref[:, h * HEAD : (h + 1) * HEAD]
            found = lax.dot_general(
                query, kv_ref[0, j], (((1,), (1,)), ((), ())), preferred_element_type=F32
            )
            if masked:
                row = lax.broadcasted_iota(jnp.int32, found.shape, 0)
                col = lax.broadcasted_iota(jnp.int32, found.shape, 1)
                found = jnp.where(col <= row, found, -jnp.inf)
            scores[h, j] = found
            tiles = [found[:, i * 128 : (i + 1) * 128] for i in range(3)]
            peak[h] = jnp.maximum(jnp.maximum(peak[h], tiles[0]), jnp.maximum(tiles[1], tiles[2]))

    def use(s, q):
        @pl.when((s == 0) & (q < own))
        def _():
            score(q, False)

    for _ in torus.run(use):
        pass
    score(own, True)
    after = own + 1

    @pl.when(lax.rem(own, 2) == 0)
    def _():
        for h in range(4):
            scores[h, after] = jnp.full((rows, rows), -jnp.inf, F32)

    for h in range(4):
        top = jnp.broadcast_to(jnp.max(peak[h], axis=1, keepdims=True) * factor, (rows, 128))

        def pair(j, carry):
            norm, total = carry
            tiles = [
                jnp.exp2(scores[h, 2 * j + i // 3, :, i % 3 * 128 : (i % 3 + 1) * 128] * factor - top)
                for i in range(6)
            ]
            norm = norm + (((tiles[0] + tiles[1]) + (tiles[2] + tiles[3])) + (tiles[4] + tiles[5]))
            weights = jnp.concatenate([tile.astype(BF16) for tile in tiles], axis=1)
            values = kv_ref[1, pl.ds(2 * j, 2)].reshape(2 * rows, HEAD)
            return norm, total + jnp.dot(weights, values, preferred_element_type=F32)

        start = (jnp.zeros((rows, 128), F32), jnp.zeros((rows, HEAD), F32))
        norm, total = lax.fori_loop(0, lax.div(own, 2) + 1, pair, start)
        cols = slice(h * HEAD, (h + 1) * HEAD)
        o_ref[:, cols] = (total / jnp.sum(norm, axis=1, keepdims=True)).astype(BF16)
    torus.finish()


def attention(queries, shard):
    rows = queries.shape[0]
    return pl.pallas_call(
        attention_kernel,
        out_shape=jax.ShapeDtypeStruct(queries.shape, BF16),
        in_specs=[VMEM, VMEM],
        out_specs=VMEM,
        scratch_shapes=[
            pltpu.VMEM((2, 16, rows, HEAD), BF16),
            pltpu.VMEM((4, 16, rows, rows), F32),
            pltpu.VMEM((4, rows, HEAD), F32),
        ]
        + torus_sems(),
        compiler_params=pltpu.CompilerParams(
            collective_id=1, has_side_effects=True, vmem_limit_bytes=60 * MIB
        ),
        name="attention",
    )(queries, shard)


def local(
    patches,
    norm_gain,
    norm_shift,
    merge_in_weight,
    merge_in_bias,
    merge_out_weight,
    merge_out_bias,
    text_embeds,
    rms_gain,
    query_weight,
    query_bias,
    key_weight,
    key_bias,
    value_weight,
    value_bias,
    patch_counts,
    image_offsets,
):
    section = lax.axis_index("section")
    own_rows = text_embeds.shape[0]
    positions = lax.axis_index("seq") * own_rows + jnp.arange(own_rows, dtype=jnp.int32)
    column = jnp.arange(HEAD, dtype=jnp.int32)
    inv_freq = jnp.exp((column % 64).astype(F32) * (-2.0 * math.log(1000000.0) / HEAD))
    angles = positions.astype(F32)[:, None] * inv_freq[None, :]
    cosine = jnp.cos(angles)
    sine = jnp.where(column < 64, -1.0, 1.0)[None, :] * jnp.sin(angles)
    key_value_bias = jnp.where(section == 0, key_bias, value_bias)
    pieces = [norm_gain, norm_shift, merge_in_bias, merge_out_bias, query_bias, key_value_bias, rms_gain]
    sizes = [piece.shape[0] for piece in pieces]
    vecs = sum(
        jnp.pad(piece.astype(F32), (sum(sizes[:i]), sum(sizes[i + 1 :])))[None, :]
        for i, piece in enumerate(pieces)
    )
    part, text_rows, text_last = merger(
        image_offsets, vecs, patches, merge_in_weight, merge_out_weight, text_embeds
    )
    queries, shard, embeds = spread(
        image_offsets,
        patch_counts,
        vecs,
        cosine,
        sine,
        part,
        text_rows,
        text_last,
        text_embeds,
        query_weight,
        key_weight,
        value_weight,
    )
    return (embeds, attention(queries, shard))


def solution(mesh):
    placed = (
        P("seq", None),
        P(),
        P(),
        P(None, ("section", "mp")),
        P(("section", "mp")),
        P(("section", "mp"), "seq"),
        P("seq"),
        P("seq", "mp"),
        P(),
        P(None, ("section", "mp")),
        P(("section", "mp")),
        P(None, "mp"),
        P("mp"),
        P(None, "mp"),
        P("mp"),
        P(),
        P(),
    )
    return jax.shard_map(
        local,
        mesh=mesh,
        in_specs=placed,
        out_specs=(P("seq", "mp"), P("seq", ("section", "mp"))),
        check_vma=False,
    )
```

```python
import math

import jax
import jax.numpy as jnp
from jax import lax
from jax.experimental import pallas as pl
from jax.experimental.pallas import tpu as pltpu
from jax.sharding import PartitionSpec as P

HEAD = 128
MESH = pl.DeviceIdType.MESH
MIB = 1024 * 1024
ANY = pl.BlockSpec(memory_space=pl.ANY)
VMEM = pl.BlockSpec(memory_space=pltpu.VMEM)
BF16 = jnp.bfloat16
F32 = jnp.float32


def coords():
    s = lax.axis_index("section")
    q = lax.axis_index("seq")
    z = lax.div(q, 4)
    y = s * 2 + lax.rem(lax.div(q, 2), 2)
    return z, y, lax.rem(q, 2), lax.axis_index("mp")


def place(z, y, c):
    return lax.div(y, 2), z * 4 + lax.rem(y, 2) * 2 + c


def device(z, y, c, x):
    s, q = place(z, y, c)
    return {"section": s, "seq": q, "mp": x}


def torus_sems():
    dma = pltpu.SemaphoreType.DMA
    return [dma((4,)), dma((4,)), dma((4, 4)), dma((4, 4)), dma((4, 4)), dma((4, 4)), dma]


class Torus:
    def __init__(self, x_ref, out_ref, sems, base, count):
        self.x_ref, self.out_ref = x_ref.at[pl.ds(base, count)], out_ref
        self.base, self.count = base, count
        self.a_send, self.a_recv, self.b_send, self.b_recv, self.s_send, self.s_recv, self.own_sem = sems
        self.z, self.y, self.c, self.x = coords()
        self.half = count // 2
        self.started = []
        self.sibling = device(self.z, self.y, 1 - self.c, self.x)

    def where(self, da, db, core):
        zz = lax.rem(self.z + da * (1 - core) + db * core + 8, 4)
        yy = lax.rem(self.y + da * core + db * (1 - core) + 8, 4)
        return place(zz, yy, core)

    def target(self, da, db):
        s, q = self.where(da, db, self.c)
        return {"section": s, "seq": q, "mp": self.x}

    def peers(self):
        return [self.target(1, 0), self.target(-1, 0), self.target(0, 1), self.target(0, -1), self.sibling]

    def view(self, da, db, core, part):
        s, q = self.where(da, db, core)
        if part is None:
            return self.out_ref.at[s, q, pl.ds(self.base, self.count)]
        return self.out_ref.at[s, q, pl.ds(self.base + part * self.half, self.half)]

    def send(self, da, db, part, send_sem, recv_sem, to):
        block = self.view(da, db, self.c, part)
        copy = pltpu.make_async_remote_copy(
            src_ref=self.x_ref if da == 0 and db == 0 else block,
            dst_ref=block,
            send_sem=send_sem,
            recv_sem=recv_sem,
            device_id=to,
            device_id_type=MESH,
        )
        copy.start()
        self.started.append(copy)

    def arrived(self, da, db, core, part, send_sem, recv_sem):
        block = self.view(da, db, core, part)
        pltpu.make_async_remote_copy(
            src_ref=block,
            dst_ref=block,
            send_sem=send_sem,
            recv_sem=recv_sem,
            device_id=self.sibling,
            device_id_type=MESH,
        ).wait_recv()

    def along_b(self, a, da):
        self.send(da, 0, None, self.b_send.at[a, 0], self.b_recv.at[a, 0], self.target(0, 1))
        self.send(da, 0, None, self.b_send.at[a, 1], self.b_recv.at[a, 1], self.target(0, -1))
        self.send(da, 0, None, self.s_send.at[a, 0], self.s_recv.at[a, 0], self.sibling)

    def start(self):
        self.send(0, 0, None, self.a_send.at[0], self.a_recv.at[0], self.target(1, 0))
        self.send(0, 0, None, self.a_send.at[1], self.a_recv.at[1], self.target(-1, 0))
        self.along_b(0, 0)
        self.own_copy = pltpu.make_async_copy(self.x_ref, self.view(0, 0, self.c, None), self.own_sem)
        self.own_copy.start()

    def run(self, use):
        offsets = [0, -1, 1, 2]
        c = self.c

        def from_sibling(a, b):
            da, db = offsets[a], offsets[b]
            self.arrived(da, db, 1 - c, None, self.s_send.at[a, b], self.s_recv.at[a, b])
            use(*self.where(da, db, 1 - c))

        def relay_b(a):
            da = offsets[a]
            self.arrived(da, -1, c, None, self.b_send.at[a, 0], self.b_recv.at[a, 0])
            self.send(da, -1, 0, self.b_send.at[a, 2], self.b_recv.at[a, 2], self.target(0, 1))
            self.send(da, -1, None, self.s_send.at[a, 1], self.s_recv.at[a, 1], self.sibling)
            self.arrived(da, 1, c, None, self.b_send.at[a, 1], self.b_recv.at[a, 1])
            self.send(da, 1, 1, self.b_send.at[a, 3], self.b_recv.at[a, 3], self.target(0, -1))
            self.send(da, 1, None, self.s_send.at[a, 2], self.s_recv.at[a, 2], self.sibling)
            use(*self.where(da, -1, c))
            use(*self.where(da, 1, c))

        self.own_copy.wait()
        use(*self.where(0, 0, c))
        self.arrived(-1, 0, c, None, self.a_send.at[0], self.a_recv.at[0])
        self.send(-1, 0, 0, self.a_send.at[2], self.a_recv.at[2], self.target(1, 0))
        self.along_b(1, -1)
        self.arrived(1, 0, c, None, self.a_send.at[1], self.a_recv.at[1])
        self.send(1, 0, 1, self.a_send.at[3], self.a_recv.at[3], self.target(-1, 0))
        self.along_b(2, 1)
        use(*self.where(-1, 0, c))
        use(*self.where(1, 0, c))
        from_sibling(0, 0)
        yield
        relay_b(0)
        yield
        self.arrived(2, 0, c, 0, self.a_send.at[2], self.a_recv.at[2])
        self.arrived(2, 0, c, 1, self.a_send.at[3], self.a_recv.at[3])
        self.along_b(3, 2)
        use(*self.where(2, 0, c))
        from_sibling(1, 0)
        from_sibling(2, 0)
        for a in (1, 2, 3):
            relay_b(a)
            from_sibling(a - 1, 1)
            from_sibling(a - 1, 2)
            yield
        from_sibling(3, 0)
        from_sibling(3, 1)
        from_sibling(3, 2)
        for a in range(4):
            da = offsets[a]
            self.arrived(da, 2, c, 0, self.b_send.at[a, 2], self.b_recv.at[a, 2])
            self.arrived(da, 2, c, 1, self.b_send.at[a, 3], self.b_recv.at[a, 3])
            self.send(da, 2, None, self.s_send.at[a, 3], self.s_recv.at[a, 3], self.sibling)
            use(*self.where(da, 2, c))
        for a in range(4):
            from_sibling(a, 3)

    def finish(self):
        for copy in self.started:
            copy.wait_send()


def greet(peers):
    barrier = pltpu.get_barrier_semaphore()
    for peer in peers:
        pl.semaphore_signal(barrier, inc=1, device_id=peer, device_id_type=MESH)
    pl.semaphore_wait(barrier, len(peers))


class CrossSum:
    def __init__(self, staged, relay, relayed, got, sums, bias, send_sem, recv_sem):
        self.staged, self.relay, self.relayed, self.got, self.sums = staged, relay, relayed, got, sums
        self.bias, self.send_sem, self.recv_sem = bias, send_sem, recv_sem
        z, y, c, x = coords()
        self.x = x
        self.right, self.left, self.across = lax.rem(x + 1, 4), lax.rem(x + 3, 4), lax.rem(x + 2, 4)
        self.to_right, self.to_left = device(z, y, c, self.right), device(z, y, c, self.left)

    def copy(self, g, i):
        top, bottom = pl.ds(0, 128), pl.ds(128, 128)
        staged, got, sums = self.staged.at[g], self.got.at[g], self.sums.at[g]
        source, target, to = [
            (staged.at[self.across, top], self.relay.at[g, 0], self.to_right),
            (staged.at[self.across, bottom], self.relay.at[g, 1], self.to_left),
            (staged.at[self.right, bottom], got.at[0, bottom], self.to_right),
            (staged.at[self.left, top], got.at[1, top], self.to_left),
            (self.relayed.at[g, 0], got.at[0, top], self.to_right),
            (self.relayed.at[g, 1], got.at[1, bottom], self.to_left),
            (sums.at[self.x], sums.at[self.x], self.to_right),
            (sums.at[self.x], sums.at[self.x], self.to_left),
            (sums.at[self.left, top], sums.at[self.left, top], self.to_right),
            (sums.at[self.right, bottom], sums.at[self.right, bottom], self.to_left),
        ][i]
        return pltpu.make_async_remote_copy(
            src_ref=source,
            dst_ref=target,
            send_sem=self.send_sem.at[g, i],
            recv_sem=self.recv_sem.at[g, i],
            device_id=to,
            device_id_type=MESH,
        )

    def landed(self, g, origin, part, i):
        block = self.sums.at[g, origin] if part is None else self.sums.at[g, origin, pl.ds(part * 128, 128)]
        pltpu.make_async_remote_copy(
            src_ref=block,
            dst_ref=block,
            send_sem=self.send_sem.at[g, i],
            recv_sem=self.recv_sem.at[g, i],
            device_id=self.to_right,
            device_id_type=MESH,
        ).wait_recv()

    def start(self, g):
        for i in range(4):
            self.copy(g, i).start()

    def pass_on(self, g):
        for i, to in ((0, self.right), (1, self.left)):
            self.copy(g, i).wait_recv()

            def body(j, carry, i=i, to=to):
                here = pl.ds(pl.multiple_of(j * 32, 32), 32)
                there = pl.ds(pl.multiple_of(j * 32 + i * 128, 32), 32)
                both = self.relay[g, i, here, :].astype(F32) + self.staged[g, to, there, :].astype(F32)
                self.relayed[g, i, here, :] = both.astype(BF16)
                return carry

            lax.fori_loop(0, 4, body, 0)
            self.copy(g, 4 + i).start()

    def add_up(self, g):
        for i in range(2, 6):
            self.copy(g, i).wait_recv()

        def body(j, carry):
            here = pl.ds(pl.multiple_of(j * 32, 32), 32)
            value = self.staged[g, self.x, here, :].astype(F32) + self.bias
            value = value + self.got[g, 0, here, :].astype(F32) + self.got[g, 1, here, :].astype(F32)
            self.sums[g, self.x, here, :] = value.astype(BF16)
            return carry

        lax.fori_loop(0, 8, body, 0)
        self.copy(g, 6).start()
        self.copy(g, 7).start()

    def spread(self, g):
        self.landed(g, self.left, None, 6)
        self.copy(g, 8).start()
        self.landed(g, self.right, None, 7)
        self.copy(g, 9).start()

    def done(self, g):
        self.landed(g, self.across, 0, 8)
        self.landed(g, self.across, 1, 9)

    def finish(self, g):
        for i in range(10):
            self.copy(g, i).wait_send()


GROUP = 32


def merger_kernel(
    offsets, vecs, patches_ref, w_in_ref, w_out_ref, text,
    part, text_rows, text_last,
    x_buf, w_in, normed, joined, shard, hidden, weight, product, staged, relay, relayed, got, sums,
    t_send, t_recv, w_sem, c_send, c_recv, *sems
):
    halves = [Torus(shard, hidden, sems[h * 7 : h * 7 + 7], h * 128, 128) for h in range(2)]
    z, y, c, x = coords()
    section = lax.div(y, 2)
    cross = CrossSum(
        staged, relay, relayed, got, sums,
        vecs[:, pl.ds(pl.multiple_of(3200 + section * 256, 128), 256)], c_send, c_recv,
    )
    load_x = [
        pltpu.make_async_copy(patches_ref.at[pl.ds(h * 512, 512)], x_buf.at[pl.ds(h * 512, 512)], w_sem.at[5 + h])
        for h in range(2)
    ]
    load_w = [
        pltpu.make_async_copy(w_in_ref.at[pl.ds(i * 1280, 1280)], w_in.at[pl.ds(i * 1280, 1280)], w_sem.at[7 + i])
        for i in range(4)
    ]
    for load in load_x + load_w:
        load.start()
    other = device(z, lax.rem(y + 2, 4), c, x)
    greet(halves[0].peers() + [device(z, y, c, lax.rem(x + d, 4)) for d in (1, 2, 3)] + [other])

    def half_of(s):
        return w_out_ref.at[:, pl.ds(pl.multiple_of(s * 256, 256), 256)]

    swap = pltpu.make_async_remote_copy(
        src_ref=half_of(1 - section),
        dst_ref=weight.at[1],
        send_sem=w_sem.at[2],
        recv_sem=w_sem.at[3],
        device_id=other,
        device_id_type=MESH,
    )
    swap.start()
    keep = pltpu.make_async_copy(half_of(section), weight.at[0], w_sem.at[4])
    keep.start()

    def text_copy(d, last):
        to = lax.rem(x + d, 4)
        if last:
            source, target = text.at[pl.ds(256, 128)], text_last.at[x]
        else:
            source, target = text.at[pl.ds(pl.multiple_of(to * 64, 64), 64)], text_rows.at[x]
        return pltpu.make_async_remote_copy(
            src_ref=source,
            dst_ref=target,
            send_sem=t_send.at[last, d],
            recv_sem=t_recv.at[last, d],
            device_id=device(z, y, c, to),
            device_id_type=MESH,
        )

    for last in (0, 1):
        for d in (1, 2, 3):
            text_copy(d, last).start()

    width = patches_ref.shape[1]
    tiles = width // 128
    gain, shift = vecs[:, :1280], vecs[:, 1280:2560]
    def norm(h, first, last):
        def body(i, carry):
            from_row = pl.ds(pl.multiple_of(h * 512 + i * 64, 64), 64)
            to_row = pl.ds(pl.multiple_of(i * 64, 64), 64)
            values = x_buf[from_row, :].astype(F32)
            center = values - jnp.mean(values, axis=-1, keepdims=True)
            spread = jnp.mean(center * center, axis=-1, keepdims=True)
            result = center * lax.rsqrt(spread + 1e-06) * gain + shift
            for u in range(tiles):
                normed[u, to_row, :] = result[:, u * 128 : (u + 1) * 128]
            return carry

        lax.fori_loop(first, last, body, 0)

    def join():
        for t in range(4):
            for u in range(tiles):
                cols = slice((t * tiles + u) * 128, (t * tiles + u + 1) * 128)
                joined[:, cols] = normed[u, pl.ds(t, 128, stride=4), :].astype(BF16)

    def multiply(h, first):
        cols = slice(first, min(first + 256, 640))
        total = jnp.dot(joined[...], w_in[:, cols], preferred_element_type=F32)
        total = total + vecs[:, 2560 + cols.start : 2560 + cols.stop]
        shard[h * 128 : (h + 1) * 128, cols] = (0.5 * total * (1.0 + lax.erf(total * (2.0**-0.5)))).astype(BF16)

    def use(h):
        def multiply_out(s, q):
            block = hidden[s, q, h * 128 : (h + 1) * 128, :]
            total = jnp.dot(block, weight[lax.rem(s + section, 2)], preferred_element_type=F32)
            rows = pl.ds(pl.multiple_of(q * 256 + h * 128, 128), 128)
            for half in range(2):
                product[half, rows, :] += total[:, half * 128 : (half + 1) * 128]

        return multiply_out

    runs = [halves[h].run(use(h)) for h in range(2)]
    load_x[0].wait()
    norm(0, 0, 8)
    join()
    for load in load_w:
        load.wait()
    for first in (0, 256, 512):
        multiply(0, first)
    halves[0].start()
    product[...] = jnp.zeros(product.shape, F32)
    load_x[1].wait()
    norm(1, 0, 8)
    keep.wait()
    swap.wait()
    next(runs[0])
    join()
    multiply(1, 0)
    next(runs[0])
    multiply(1, 256)
    multiply(1, 512)
    next(runs[0])
    next(runs[0])
    halves[1].start()
    for _ in runs[0]:
        pass

    def rows_of(g, n, m):
        return pl.ds((g % 2 * 8 + n) * 256 + g // 2 * 128 + m * 32, 32)

    def stage(g):
        for n in range(8):
            for m in range(4):
                for half in range(2):
                    cols = slice(half * 128, (half + 1) * 128)
                    staged[g, m, n * 32 : (n + 1) * 32, cols] = product[half, rows_of(g, n, m), :].astype(BF16)
        cross.start(g)

    def unstage(g):
        cross.done(g)
        for n in range(8):
            for m in range(4):
                for half in range(2):
                    cols = slice(half * 128, (half + 1) * 128)
                    product[half, rows_of(g, n, m), :] = sums[g, m, n * 32 : (n + 1) * 32, cols].astype(F32)

    stage(0)
    stage(1)
    next(runs[1])
    next(runs[1])
    cross.pass_on(0)
    cross.pass_on(1)
    next(runs[1])
    next(runs[1])
    cross.add_up(0)
    cross.add_up(1)
    next(runs[1])
    cross.spread(0)
    cross.spread(1)
    for _ in runs[1]:
        pass
    stage(2)
    stage(3)
    cross.pass_on(2)
    cross.pass_on(3)
    unstage(0)
    unstage(1)
    cross.add_up(2)
    cross.add_up(3)
    cross.spread(2)
    cross.spread(3)
    unstage(2)
    unstage(3)
    row = lax.broadcasted_iota(jnp.int32, (GROUP, 128), 0)

    def body(q, image_a):
        for i in range(12):
            k, m = (i % 2, i // 2) if i < 8 else (2, i - 8)
            first = q * 384 + i * GROUP
            following = jnp.minimum(image_a + 1, 15)
            image_a = jnp.where(offsets[following] <= first, following, image_a)
            image_b = jnp.minimum(image_a + 1, 15)
            begin = jnp.where(image_a == 15, GROUP, jnp.clip(offsets[image_b] - first, 0, GROUP))
            start_a = jnp.clip(image_a * 256 + first - offsets[image_a], 0, 4096)
            start_b = jnp.clip(image_b * 256 - begin, 0, 4096)
            for half in range(2):
                one = product[half, pl.ds(start_a, GROUP), :]
                two = product[half, pl.ds(start_b, GROUP), :]
                cols = slice(half * 128, (half + 1) * 128)
                part[k, q, m, :, cols] = jnp.where(row >= begin, two, one).astype(BF16)
        return image_a

    lax.fori_loop(0, 16, body, jnp.int32(0))
    for torus in halves:
        torus.finish()
    for g in range(4):
        cross.finish(g)
    for last, target in ((0, text_rows), (1, text_last)):
        for d in (1, 2, 3):
            block = target.at[lax.rem(x + 4 - d, 4)]
            pltpu.make_async_remote_copy(
                src_ref=block,
                dst_ref=block,
                send_sem=t_send.at[last, d],
                recv_sem=t_recv.at[last, d],
                device_id=other,
                device_id_type=MESH,
            ).wait_recv()
            text_copy(d, last).wait_send()


def merger(offsets, vecs, patches, w_in, w_out, text):
    dma = pltpu.SemaphoreType.DMA
    return pl.pallas_call(
        merger_kernel,
        in_specs=[pl.BlockSpec(memory_space=pltpu.SMEM), VMEM, ANY, ANY, ANY, ANY],
        out_specs=[VMEM, ANY, ANY],
        out_shape=[
            jax.ShapeDtypeStruct((3, 16, 4, GROUP, 256), BF16),
            jax.ShapeDtypeStruct((4, 64, 2048), BF16),
            jax.ShapeDtypeStruct((4, 128, 2048), BF16),
        ],
        scratch_shapes=[
            pltpu.VMEM((1024, 1280), BF16),
            pltpu.VMEM((5120, 640), BF16),
            pltpu.VMEM((10, 512, 128), F32),
            pltpu.VMEM((128, 5120), BF16),
            pltpu.VMEM((256, 640), BF16),
            pltpu.VMEM((2, 16, 256, 640), BF16),
            pltpu.VMEM((2, 640, 256), BF16),
            pltpu.VMEM((2, 4096 + GROUP, 128), F32),
            pltpu.VMEM((4, 4, 256, 256), BF16),
            pltpu.VMEM((4, 2, 128, 256), BF16),
            pltpu.VMEM((4, 2, 128, 256), BF16),
            pltpu.VMEM((4, 2, 256, 256), BF16),
            pltpu.VMEM((4, 4, 256, 256), BF16),
            dma((2, 4)),
            dma((2, 4)),
            dma((11,)),
            dma((4, 10)),
            dma((4, 10)),
        ]
        + torus_sems()
        + torus_sems(),
        compiler_params=pltpu.CompilerParams(
            collective_id=0, has_side_effects=True, vmem_limit_bytes=60 * MIB
        ),
        name="merger",
    )(offsets, vecs, patches, w_in, w_out, text)


def spread_kernel(
    offsets, counts, vecs, cos_ref, sin_ref, part, text_ref, text_last_ref, own_text, wq_ref, wk_ref, wv_ref,
    q_out, kv_out, e_hbm,
    e_out, rows, rows_last, text, text_last, out, normed, wq, wkv, total,
    v_send, v_recv, own_sem, g_send, g_recv, load_sem, text_sem,
):
    z, y, c, x = coords()
    s, q = place(z, y, c)
    linear = s * 16 + q
    right, left, across = lax.rem(x + 1, 4), lax.rem(x + 3, 4), lax.rem(x + 2, 4)
    to_right, to_left = device(z, y, c, right), device(z, y, c, left)
    load_text, load_last = [], []
    for d in range(4):
        slot = lax.rem(x + d, 4)
        near, last = text_ref.at[slot], text_last_ref.at[slot]
        if d == 0:
            near = own_text.at[pl.ds(pl.multiple_of(x * 64, 64), 64)]
            last = own_text.at[pl.ds(256, 128)]
        load_text.append(pltpu.make_async_copy(near, text.at[slot], text_sem.at[0, d]))
        load_last.append(pltpu.make_async_copy(last, text_last.at[slot], text_sem.at[1, d]))
    load_q = pltpu.make_async_copy(wq_ref, wq, load_sem.at[1])
    for load in load_text + load_last + [load_q]:
        load.start()

    @pl.when(s == 0)
    def _():
        pltpu.make_async_copy(wk_ref, wkv, load_sem.at[2]).start()

    @pl.when(s == 1)
    def _():
        pltpu.make_async_copy(wv_ref, wkv, load_sem.at[2]).start()

    def peer(j):
        other = lax.rem(linear + j, 32)
        return lax.div(other, 16), lax.rem(other, 16)

    barrier = pltpu.get_barrier_semaphore()
    for to in (to_right, to_left):
        pl.semaphore_signal(barrier, inc=1, device_id=to, device_id_type=MESH)

    def hello(j, carry):
        ps, pq = peer(j)
        pl.semaphore_signal(
            barrier, inc=1, device_id={"section": ps, "seq": pq, "mp": x}, device_id_type=MESH
        )
        return carry

    lax.fori_loop(1, 32, hello, 0)
    pl.semaphore_wait(barrier, 33)

    def own_copy(k):
        if k < 2:
            return pltpu.make_async_copy(part.at[k, q, x], rows.at[k, q * 2 + s], own_sem.at[k])
        return pltpu.make_async_copy(part.at[k, q], rows_last.at[q * 2 + s], own_sem.at[k])

    def start_owner(k):
        def body(j, carry):
            ps, pq = peer(j)
            pltpu.make_async_remote_copy(
                src_ref=part.at[k, pq, x] if k < 2 else part.at[k, pq],
                dst_ref=rows.at[k, q * 2 + s] if k < 2 else rows_last.at[q * 2 + s],
                send_sem=v_send.at[k],
                recv_sem=v_recv.at[k],
                device_id={"section": ps, "seq": pq, "mp": x},
                device_id_type=MESH,
            ).start()
            return carry

        lax.fori_loop(1, 32, body, 0)
        own_copy(k).start()

    def visual_rows(first):
        position = q * 384 + first + lax.broadcasted_iota(jnp.int32, (GROUP, 256), 0)
        found = jnp.zeros((GROUP, 256), jnp.int32)
        for i in range(16):
            begin = offsets[i]
            inside = (position >= begin) & (position < begin + lax.div(counts[i], 4))
            found = jnp.where(inside, 1, found)
        return found > 0

    def others(k):
        return rows.at[k, pl.ds(0, 31)] if k < 2 else rows_last.at[pl.ds(0, 31)]

    def place_rows(k):
        own_copy(k).wait()
        pltpu.make_async_copy(others(k), others(k), v_recv.at[k]).wait()
        if k < 2:
            visual = visual_rows(x * 64 + k * 32)
            for b in range(32):
                own_text = text[b // 8, k * 32 : (k + 1) * 32, (b % 8) * 256 : (b % 8 + 1) * 256]
                out[k, x, b] = jnp.where(visual, rows[k, b].astype(F32), own_text.astype(F32)).astype(BF16)
        else:
            for m in range(4):
                visual = visual_rows(256 + m * 32)
                for b in range(32):
                    own_text = text_last[b // 8, m * 32 : (m + 1) * 32, (b % 8) * 256 : (b % 8 + 1) * 256]
                    picked = jnp.where(visual, rows_last[b, m].astype(F32), own_text.astype(F32))
                    out[k, m, b] = picked.astype(BF16)

    def row_copy(k, piece, origin, to, slot):
        block = out.at[k, origin] if piece is None else out.at[k, origin, pl.ds(piece * 16, 16)]
        return pltpu.make_async_remote_copy(
            src_ref=block,
            dst_ref=block,
            send_sem=g_send.at[k, slot],
            recv_sem=g_recv.at[k, slot],
            device_id=to,
            device_id_type=MESH,
        )

    def start_rows(k):
        row_copy(k, None, x, to_right, 0).start()
        row_copy(k, None, x, to_left, 1).start()

    def relay_rows(k):
        row_copy(k, None, left, to_right, 0).wait_recv()
        row_copy(k, 0, left, to_right, 2).start()
        row_copy(k, None, right, to_left, 1).wait_recv()
        row_copy(k, 1, right, to_left, 3).start()

    def project(k):
        if k < 2:
            row_copy(k, 0, across, to_right, 2).wait_recv()
            row_copy(k, 1, across, to_left, 3).wait_recv()

        def square(b, carry):
            values = out[k, :, b].reshape(128, 256).astype(F32)
            return carry + values * values

        squares = lax.fori_loop(0, 32, square, jnp.zeros((128, 256), F32), unroll=2)
        mean = jnp.sum(squares, axis=-1, keepdims=True) * (1.0 / 8192.0)
        scale = jnp.broadcast_to(lax.rsqrt(mean + 1e-06), (128, 256))

        total[...] = jnp.broadcast_to(vecs[:, 3712:4352], total.shape)

        def depth(i, carry):
            for j in range(4):
                b = i * 4 + j
                values = out[k, :, b].reshape(128, 256).astype(F32)
                gain = vecs[:, pl.ds(pl.multiple_of(4352 + b * 256, 128), 256)]
                normed[:, j * 256 : (j + 1) * 256] = (values * scale * gain).astype(BF16)
            span = pl.ds(pl.multiple_of(i * 1024, 1024), 1024)
            total[:, :512] += jnp.dot(normed[...], wq[span, :], preferred_element_type=F32)
            total[:, 512:] += jnp.dot(normed[...], wkv[span, :], preferred_element_type=F32)
            return carry

        lax.fori_loop(0, 8, depth, 0)
        for m in range(4):
            here = slice(m * 32, (m + 1) * 32)
            there = pl.ds(m * 64 + k * 32 if k < 2 else 256 + m * 32, 32)
            cosine, sine = cos_ref[there, :], sin_ref[there, :]

            def rotate(values):
                return (values * cosine + pltpu.roll(values, 64, 1) * sine).astype(BF16)

            for h in range(4):
                cols = slice(h * 128, (h + 1) * 128)
                q_out[there, cols] = rotate(total[here, cols])

            @pl.when(s == 0)
            def _():
                kv_out[there, :] = rotate(total[here, 512:])

            @pl.when(s == 1)
            def _():
                kv_out[there, :] = total[here, 512:].astype(BF16)

            for j in range(8):
                e_out[there, j * 256 : (j + 1) * 256] = out[k, m, x * 8 + j]

    for k in range(3):
        start_owner(k)
    for load in load_text:
        load.wait()
    place_rows(0)
    start_rows(0)
    place_rows(1)
    start_rows(1)
    relay_rows(0)
    relay_rows(1)
    load_q.wait()
    pltpu.make_async_copy(wk_ref, wkv, load_sem.at[2]).wait()
    project(0)
    for load in load_last:
        load.wait()
    place_rows(2)
    project(2)
    project(1)
    save = pltpu.make_async_copy(e_out, e_hbm, load_sem.at[4])
    save.start()
    for k in range(3):
        pltpu.make_async_copy(others(k), others(k), v_send.at[k]).wait()
    for k in range(2):
        row_copy(k, None, x, to_right, 0).wait_send()
        row_copy(k, None, x, to_left, 1).wait_send()
        row_copy(k, 0, left, to_right, 2).wait_send()
        row_copy(k, 1, right, to_left, 3).wait_send()
    save.wait()


def spread(offsets, counts, vecs, cos, sin, part, text, text_last, own_text, wq, wk, wv):
    dma = pltpu.SemaphoreType.DMA
    smem = pl.BlockSpec(memory_space=pltpu.SMEM)
    return pl.pallas_call(
        spread_kernel,
        out_shape=[
            jax.ShapeDtypeStruct((384, 512), BF16),
            jax.ShapeDtypeStruct((384, 128), BF16),
            jax.ShapeDtypeStruct((384, 2048), BF16),
        ],
        in_specs=[smem, smem, VMEM, VMEM, VMEM, VMEM] + [ANY] * 6,
        out_specs=[VMEM, VMEM, ANY],
        scratch_shapes=[
            pltpu.VMEM((384, 2048), BF16),
            pltpu.VMEM((2, 32, GROUP, 256), BF16),
            pltpu.VMEM((32, 4, GROUP, 256), BF16),
            pltpu.VMEM((4, 64, 2048), BF16),
            pltpu.VMEM((4, 128, 2048), BF16),
            pltpu.VMEM((3, 4, 32, GROUP, 256), BF16),
            pltpu.VMEM((128, 1024), BF16),
            pltpu.VMEM((8192, 512), BF16),
            pltpu.VMEM((8192, 128), BF16),
            pltpu.VMEM((128, 640), F32),
            dma((3,)),
            dma((3,)),
            dma((3,)),
            dma((2, 4)),
            dma((2, 4)),
            dma((5,)),
            dma((2, 4)),
        ],
        compiler_params=pltpu.CompilerParams(
            collective_id=2, has_side_effects=True, vmem_limit_bytes=60 * MIB
        ),
        name="spread",
    )(offsets, counts, vecs, cos, sin, part, text, text_last, own_text, wq, wk, wv)


def attention_kernel(q_ref, shard, o_ref, kv_ref, scores, peak, *sems):
    torus = Torus(shard, kv_ref, sems, 0, shard.shape[0])
    greet(torus.peers())
    torus.start()
    own = lax.axis_index("seq")
    rows = q_ref.shape[0]
    factor = HEAD**-0.5 * math.log2(math.e)
    peak[...] = jnp.full(peak.shape, -jnp.inf, F32)

    def score(j, masked):
        for h in range(4):
            query = q_ref[:, h * HEAD : (h + 1) * HEAD]
            found = lax.dot_general(
                query, kv_ref[0, j], (((1,), (1,)), ((), ())), preferred_element_type=F32
            )
            if masked:
                row = lax.broadcasted_iota(jnp.int32, found.shape, 0)
                col = lax.broadcasted_iota(jnp.int32, found.shape, 1)
                found = jnp.where(col <= row, found, -jnp.inf)
            scores[h, j] = found
            tiles = [found[:, i * 128 : (i + 1) * 128] for i in range(3)]
            peak[h] = jnp.maximum(jnp.maximum(peak[h], tiles[0]), jnp.maximum(tiles[1], tiles[2]))

    def use(s, q):
        @pl.when((s == 0) & (q < own))
        def _():
            score(q, False)

    for _ in torus.run(use):
        pass
    score(own, True)
    after = own + 1

    @pl.when(lax.rem(own, 2) == 0)
    def _():
        for h in range(4):
            scores[h, after] = jnp.full((rows, rows), -jnp.inf, F32)

    for h in range(4):
        top = jnp.broadcast_to(jnp.max(peak[h], axis=1, keepdims=True) * factor, (rows, 128))

        def pair(j, carry):
            norm, total = carry
            tiles = [
                jnp.exp2(scores[h, 2 * j + i // 3, :, i % 3 * 128 : (i % 3 + 1) * 128] * factor - top)
                for i in range(6)
            ]
            norm = norm + (((tiles[0] + tiles[1]) + (tiles[2] + tiles[3])) + (tiles[4] + tiles[5]))
            weights = jnp.concatenate([tile.astype(BF16) for tile in tiles], axis=1)
            values = kv_ref[1, pl.ds(2 * j, 2)].reshape(2 * rows, HEAD)
            return norm, total + jnp.dot(weights, values, preferred_element_type=F32)

        start = (jnp.zeros((rows, 128), F32), jnp.zeros((rows, HEAD), F32))
        norm, total = lax.fori_loop(0, lax.div(own, 2) + 1, pair, start)
        cols = slice(h * HEAD, (h + 1) * HEAD)
        o_ref[:, cols] = (total / jnp.sum(norm, axis=1, keepdims=True)).astype(BF16)
    torus.finish()


def attention(queries, shard):
    rows = queries.shape[0]
    return pl.pallas_call(
        attention_kernel,
        out_shape=jax.ShapeDtypeStruct(queries.shape, BF16),
        in_specs=[VMEM, VMEM],
        out_specs=VMEM,
        scratch_shapes=[
            pltpu.VMEM((2, 16, rows, HEAD), BF16),
            pltpu.VMEM((4, 16, rows, rows), F32),
            pltpu.VMEM((4, rows, HEAD), F32),
        ]
        + torus_sems(),
        compiler_params=pltpu.CompilerParams(
            collective_id=1, has_side_effects=True, vmem_limit_bytes=60 * MIB
        ),
        name="attention",
    )(queries, shard)


def local(
    patches,
    norm_gain,
    norm_shift,
    merge_in_weight,
    merge_in_bias,
    merge_out_weight,
    merge_out_bias,
    text_embeds,
    rms_gain,
    query_weight,
    query_bias,
    key_weight,
    key_bias,
    value_weight,
    value_bias,
    patch_counts,
    image_offsets,
):
    section = lax.axis_index("section")
    own_rows = text_embeds.shape[0]
    positions = lax.axis_index("seq") * own_rows + jnp.arange(own_rows, dtype=jnp.int32)
    column = jnp.arange(HEAD, dtype=jnp.int32)
    inv_freq = jnp.exp((column % 64).astype(F32) * (-2.0 * math.log(1000000.0) / HEAD))
    angles = positions.astype(F32)[:, None] * inv_freq[None, :]
    cosine = jnp.cos(angles)
    sine = jnp.where(column < 64, -1.0, 1.0)[None, :] * jnp.sin(angles)
    key_value_bias = jnp.where(section == 0, key_bias, value_bias)
    pieces = [norm_gain, norm_shift, merge_in_bias, merge_out_bias, query_bias, key_value_bias, rms_gain]
    sizes = [piece.shape[0] for piece in pieces]
    vecs = sum(
        jnp.pad(piece.astype(F32), (sum(sizes[:i]), sum(sizes[i + 1 :])))[None, :]
        for i, piece in enumerate(pieces)
    )
    part, text_rows, text_last = merger(
        image_offsets, vecs, patches, merge_in_weight, merge_out_weight, text_embeds
    )
    queries, shard, embeds = spread(
        image_offsets,
        patch_counts,
        vecs,
        cosine,
        sine,
        part,
        text_rows,
        text_last,
        text_embeds,
        query_weight,
        key_weight,
        value_weight,
    )
    return (embeds, attention(queries, shard))


def solution(mesh):
    placed = (
        P("seq", None),
        P(),
        P(),
        P(None, ("section", "mp")),
        P(("section", "mp")),
        P(("section", "mp"), "seq"),
        P("seq"),
        P("seq", "mp"),
        P(),
        P(None, ("section", "mp")),
        P(("section", "mp")),
        P(None, "mp"),
        P("mp"),
        P(None, "mp"),
        P("mp"),
        P(),
        P(),
    )
    return jax.shard_map(
        local,
        mesh=mesh,
        in_specs=placed,
        out_specs=(P("seq", "mp"), P("seq", ("section", "mp"))),
        check_vma=False,
    )
```
